32 devices in a mesh: tiles: 2 (over y), strip: 4 (over z), col: 2 (over x), expo: 2 (over core).
Axes of the slice: x: 2, y: 2, z: 4, core: 2. Of those that a mesh axis runs over, the one named last changes fastest.
Arguments:
- mask_params: float32 [2, 2048, 256], P('expo', ('tiles', 'strip'), 'col'), parts along dimension 1, may hold values from -3 to 3
- target: int32 [2048, 256], P(('tiles', 'strip'), 'col'), parts along dimension 0, may hold values from 0 to 1, as said below
- col_taps: bfloat16 [24, 2, 65], replicated, may hold values from -0.75 to 0.75
- row_taps: bfloat16 [24, 2, 65], replicated, may hold values from -0.75 to 0.75
- kernel_weights: float32 [24], replicated, may hold values from 0.05 to 0.5
Outputs:
- new_params: float32 [2, 2048, 256], P('expo', ('tiles', 'strip'), 'col'), parts along dimension 1
- resist: float32 [2048, 256], P(('tiles', 'strip'), 'col'), parts along dimension 0
- mean_loss: float32 [2], P('tiles'), parts along dimension 0
The draws below stay inside these ranges and needn't reach their ends.
There are 2 independent parts, one for each index of `tiles`. The reference program is written for one: setup_inputs(seed, part) draws one part's arguments, and reference() takes and returns one part's arrays. A program takes and returns all parts, laid end to end along the dimension named above; an argument that names none is the same for every part. Nothing has to cross between parts.
Inputs may be any that keep to these rules, and one draw needn't show every extreme that they name: `target`: 1 where the layout is printed, 0 elsewhere.
All inputs are finite; a program needn't handle non-finite values.
Results may differ from the reference program's by a relative error of at most 0.0078.
Values may be sent and summed in bfloat16 or wider, within the bound.
A program may use at most 64 MiB of HBM per device.

```python
import math
import jax
import jax.numpy as jnp
from jax import lax

TAPS = 65
KERNELS = 24
EXPOSURES = 2
HALF = 32
HEIGHT = 1024
WIDTH = 256


def draw_target(key, part):
    row_ids = jnp.arange(HEIGHT, dtype=jnp.int32)[:, None]
    level = 150 + 600 * row_ids // HEIGHT
    votes = jax.random.randint(key, (HEIGHT, WIDTH), 0, 1000, dtype=jnp.int32)
    return jnp.where(votes < level, 1, 0).astype(jnp.int32)


def levels(own_key, dims, shards, low, largest):
    gain, own = 1.0, jax.random.fold_in(own_key, 6)
    for dim, blocks in shards:
        steps = jnp.exp(jax.random.uniform(jax.random.fold_in(own, dim), (blocks,), jnp.float32, low / len(shards), largest / len(shards)))
        gain = gain * jnp.repeat(steps, dims[dim] // blocks).reshape([-1 if axis == dim else 1 for axis in range(len(dims))])
    return gain


def noise(rng, shape, deviation, most, cuts=(), held_as=jnp.bfloat16):
    drawn = deviation * jax.random.normal(rng, shape, jnp.float32)
    if cuts:
        drawn = drawn * levels(rng, shape, cuts, -0.22, 0.18)
    return jnp.clip(drawn, -most, most).astype(held_as)


def setup_inputs(seed: int = 0, part: int = 0) -> dict:
    key_list = jax.random.split(jax.random.key(seed), 6)
    own_keys = jax.random.split(jax.random.fold_in(key_list[5], part), 6)
    return {
        "mask_params": noise(own_keys[0], (EXPOSURES, HEIGHT, WIDTH), 0.5, 3.0, ((0, 2), (1, 4), (2, 2)), jnp.float32),
        "target": draw_target(jax.random.fold_in(jax.random.fold_in(key_list[5], part), 71), part),
        "col_taps": noise(key_list[2], (KERNELS, 2, TAPS), TAPS ** -0.5, 0.75),
        "row_taps": noise(key_list[3], (KERNELS, 2, TAPS), TAPS ** -0.5, 0.75),
        "kernel_weights": jnp.clip(jnp.exp(jax.random.uniform(key_list[4], (KERNELS,), jnp.float32, math.log(0.05), math.log(0.5))), 0.05, 0.5),
    }


mask_slope = 4.0
resist_steep = 4.0
resist_level = 3.0
step_length = 0.5
norm_eps = 1e-06

def conv_plane(source, kernel, pad_rows, pad_cols):
    return lax.conv_general_dilated(source.astype(jnp.float32), kernel.astype(jnp.float32), (1, 1), ((pad_rows, pad_rows), (pad_cols, pad_cols)), dimension_numbers=('NCHW', 'OIHW', 'NCHW'), precision=lax.Precision.HIGHEST)

def kernel_fields(mask_half, col_pair, row_pair):
    columns = conv_plane(mask_half, col_pair[:, None, None, :], 0, HALF).astype(jnp.bfloat16)
    height, width = (columns.shape[2], columns.shape[3])
    stacked = columns.reshape(columns.shape[0] * 2, 1, height, width)
    pair_sums = conv_plane(stacked, row_pair[:, None, :, None], HALF, 0).reshape(columns.shape[0], 2, 2, height, width)
    real_part = pair_sums[:, 0, 0] - pair_sums[:, 1, 1]
    imag_part = pair_sums[:, 0, 1] + pair_sums[:, 1, 0]
    return (real_part, imag_part)

def reference(mask_params, target, col_taps, row_taps, kernel_weights):
    mask_field = jax.nn.sigmoid(mask_slope * mask_params)
    mask_half = mask_field.astype(jnp.bfloat16)[:, None]
    kernel_ids = jnp.arange(KERNELS, dtype=jnp.int32)

    def add_intensity(running, kernel):
        real_part, imag_part = kernel_fields(mask_half, col_taps[kernel], row_taps[kernel])
        return (running + kernel_weights[kernel] * (real_part * real_part + imag_part * imag_part), None)
    intensity, unused = lax.scan(add_intensity, jnp.zeros(mask_params.shape, jnp.float32), kernel_ids)
    summed = intensity[0] + intensity[1]
    resist = jax.nn.sigmoid(resist_steep * (summed - resist_level))
    mismatch = resist - target.astype(jnp.float32)
    mean_loss = jnp.mean(mismatch * mismatch).reshape(1)
    slope_field = 2.0 * mismatch * resist_steep * resist * (1.0 - resist)
    height, width = target.shape

    def add_gradient(running, kernel):
        col_pair = col_taps[kernel]
        row_pair = row_taps[kernel]
        real_part, imag_part = kernel_fields(mask_half, col_pair, row_pair)
        weighting = 2.0 * kernel_weights[kernel] * slope_field
        products = jnp.stack([weighting * real_part, weighting * imag_part], axis=1).astype(jnp.bfloat16)
        returned = conv_plane(products.reshape(-1, 1, height, width), row_pair[:, ::-1][:, None, :, None], HALF, 0)
        returned = returned.reshape(products.shape[0], 2, 2, height, width)
        unrolled = jnp.stack([returned[:, 0, 0] + returned[:, 1, 1], returned[:, 1, 0] - returned[:, 0, 1]], axis=1).astype(jnp.bfloat16)
        term = conv_plane(unrolled, col_pair[:, ::-1][None, :, None, :], 0, HALF)[:, 0]
        return (running + term, None)
    descent, unused = lax.scan(add_gradient, jnp.zeros(mask_params.shape, jnp.float32), kernel_ids)
    gradient = descent * mask_slope * mask_field * (1.0 - mask_field)
    root_mean = jnp.sqrt(jnp.mean(gradient * gradient) + norm_eps)
    new_params = mask_params - step_length * gradient / root_mean
    return (new_params, resist, mean_loss)
```

```python
import functools

import jax
import jax.numpy as jnp
from jax import lax
from jax.experimental import pallas as pl
from jax.experimental.pallas import tpu as pltpu
from jax.sharding import PartitionSpec as P

mask_slope = 4.0
resist_steep = 4.0
resist_level = 3.0
step_length = 0.5
norm_eps = 1e-06

MESH = pl.DeviceIdType.MESH
F32 = jnp.float32
BF16 = jnp.bfloat16
WINDOW = 256
DIRECTIONS = [(a, b) for a in (-1, 0, 1) for b in (-1, 0, 1) if (a, b) != (0, 0)]


def blocks_of(total_out, reach):
    most = WINDOW - reach
    count = -(-total_out // most)
    size = -(-total_out // (count * 16)) * 16
    found = []
    for start in range(0, total_out, size):
        rows = min(size, total_out - start)
        window = min(start, total_out + reach - WINDOW)
        found.append((start, rows, window, start - window))
    return found


def dot(a, b):
    return jnp.dot(a, b, preferred_element_type=F32)


def dot_t(a, b):
    return lax.dot_general(a, b, (((1,), (1,)), ((), ())), preferred_element_type=F32)


def body(
    sizes,
    params_ref,
    target_ref,
    vec_ref,
    weight_ref,
    new_ref,
    resist_ref,
    loss_ref,
    halo,
    ext,
    col_mats,
    fwd_mats,
    adj_mats,
    columns,
    fields,
    intensity,
    other,
    slope,
    descent,
    partial,
    slots,
    halo_send,
    halo_recv,
    expo_send,
    expo_recv,
    sum_send,
    sum_recv,
):
    strips, cols, expos, half = sizes
    kernels = vec_ref.shape[0]
    rows, width = target_ref.shape
    two = 2 * half
    wide = width + 2 * two
    group = strips * cols * expos
    strip, col, expo = (lax.axis_index("strip"), lax.axis_index("col"), lax.axis_index("expo"))
    me = (strip * cols + col) * expos + expo

    def device(index):
        return {
            "strip": index // (cols * expos),
            "col": (index // expos) % cols,
            "expo": index % expos,
        }

    halo[...] = jnp.zeros_like(halo)

    barrier = pltpu.get_barrier_semaphore()

    def greet(step, carry):
        pl.semaphore_signal(
            barrier, inc=1, device_id=device(lax.rem(me + step, group)), device_id_type=MESH
        )
        return carry

    lax.fori_loop(1, group, greet, 0)

    mask = jax.nn.sigmoid(mask_slope * params_ref[0])
    halo[0, two : two + rows, width : 2 * width] = mask.astype(BF16)
    halo[1, two : two + rows, width : 2 * width] = target_ref[...].astype(F32).astype(BF16)

    def transfer(number):
        down, right = DIRECTIONS[number]
        source = {-1: (two, two), 0: (two, rows), 1: (rows, two)}[down]
        landing = {-1: two + rows, 0: two, 1: 0}[down]
        lane = {-1: 2 * width, 0: width, 1: 0}[right]
        return pltpu.make_async_remote_copy(
            src_ref=halo.at[:, pl.ds(source[0], source[1]), pl.ds(width, width)],
            dst_ref=halo.at[:, pl.ds(landing, source[1]), pl.ds(lane, width)],
            send_sem=halo_send.at[number],
            recv_sem=halo_recv.at[number],
            device_id={
                "strip": jnp.clip(strip + down, 0, strips - 1),
                "col": jnp.clip(col + right, 0, cols - 1),
            },
            device_id_type=MESH,
        )

    def inside(down, right):
        to_strip, to_col = (strip + down, col + right)
        return (to_strip >= 0) & (to_strip < strips) & (to_col >= 0) & (to_col < cols)

    pl.semaphore_wait(barrier, group - 1)

    for number, (down, right) in enumerate(DIRECTIONS):

        @pl.when(inside(down, right))
        def _():
            transfer(number).start()

    def spread(k, row, count):
        line = vec_ref[k, row : row + 1, :]
        return pltpu.roll(
            jnp.broadcast_to(line, (count, line.shape[1])), 0, 1, stride=1, stride_axis=0
        )

    span = fwd_mats.shape[2]

    def build(k, carry):
        for part in range(2):
            col_mats[k, part] = spread(k, part, wide).astype(BF16)
        t0, t1 = (spread(k, 2, span), spread(k, 3, span))
        fwd_mats[k, 0, :, :WINDOW] = t0.astype(BF16)
        fwd_mats[k, 0, :, WINDOW:] = (-t1).astype(BF16)
        fwd_mats[k, 1, :, :WINDOW] = t1.astype(BF16)
        fwd_mats[k, 1, :, WINDOW:] = t0.astype(BF16)
        g0, g1 = (spread(k, 4, span), spread(k, 5, span))
        adj_mats[k, 0, :, :WINDOW] = g0.astype(BF16)
        adj_mats[k, 0, :, WINDOW:] = g1.astype(BF16)
        adj_mats[k, 1, :, :WINDOW] = (-g1).astype(BF16)
        adj_mats[k, 1, :, WINDOW:] = g0.astype(BF16)
        return carry

    lax.fori_loop(0, kernels, build, 0)
    intensity[...] = jnp.zeros_like(intensity)
    descent[...] = jnp.zeros_like(descent)

    for number, (down, right) in enumerate(DIRECTIONS):

        @pl.when(inside(down, right))
        def _():
            transfer(number).wait_send()

        @pl.when(inside(-down, -right))
        def _():
            transfer(number).wait_recv()

    lanes = halo.shape[2]
    shifted = pltpu.roll(halo[0].astype(F32), lanes - (width - two), 1)
    ext[...] = shifted[:, :wide].astype(BF16)

    def forward(k, carry):
        for part in range(2):
            columns[part] = dot(ext[...], col_mats[k, part]).astype(BF16)
        weight = weight_ref[k]
        for start, count, window, offset in blocks_of(rows + two, two):
            source = jnp.concatenate(
                [columns[0, window : window + WINDOW, :], columns[1, window : window + WINDOW, :]],
                axis=0,
            )
            real_part = dot(fwd_mats[k, 0, offset : offset + count, :], source)
            imag_part = dot(fwd_mats[k, 1, offset : offset + count, :], source)
            fields[k, 0, start : start + count, :] = real_part
            fields[k, 1, start : start + count, :] = imag_part
            intensity[start : start + count, :] += weight * (
                real_part * real_part + imag_part * imag_part
            )
        return carry

    lax.fori_loop(0, kernels, forward, 0)

    swap = pltpu.make_async_remote_copy(
        src_ref=intensity,
        dst_ref=other,
        send_sem=expo_send,
        recv_sem=expo_recv,
        device_id={"expo": 1 - expo},
        device_id_type=MESH,
    )
    swap.start()
    swap.wait()

    tall = rows + two
    resist = jax.nn.sigmoid(resist_steep * (intensity[...] + other[...] - resist_level))
    target_ext = pltpu.roll(
        halo[1, half : half + tall, :].astype(F32), lanes - (width - half), 1
    )[:, :wide]
    row_ids = lax.broadcasted_iota(jnp.int32, (tall, wide), 0) + (strip * rows - half)
    lane_ids = lax.broadcasted_iota(jnp.int32, (tall, wide), 1)
    col_ids = lane_ids + (col * width - half)
    kept = (
        (row_ids >= 0)
        & (row_ids < strips * rows)
        & (col_ids >= 0)
        & (col_ids < cols * width)
        & (lane_ids < width + two)
    )
    mismatch = resist - target_ext
    slope[...] = jnp.where(kept, 2.0 * mismatch * resist_steep * resist * (1.0 - resist), 0.0)
    own = pltpu.roll(resist[half : half + rows, :], wide - half, 1)[:, :width]
    resist_ref[...] = own
    own_miss = own - target_ref[...].astype(F32)
    loss_line = jnp.sum(own_miss * own_miss, axis=0, keepdims=True)

    def backward(k, carry):
        weighting = (2.0 * weight_ref[k]) * slope[...]
        products = [(weighting * fields[k, part]).astype(BF16) for part in range(2)]
        taps = jnp.concatenate(
            [col_mats[k, part, two : two + width, :] for part in range(2)], axis=1
        )
        for start, count, window, offset in blocks_of(rows, two):
            source = jnp.concatenate(
                [products[part][window : window + WINDOW, :] for part in range(2)], axis=0
            )
            returned = jnp.concatenate(
                [
                    dot(adj_mats[k, part, offset : offset + count, :], source).astype(BF16)
                    for part in range(2)
                ],
                axis=1,
            )
            descent[start : start + count, :] += dot_t(returned, taps)
        return carry

    lax.fori_loop(0, kernels, backward, 0)

    mask = jax.nn.sigmoid(mask_slope * params_ref[0])
    gradient = descent[...] * mask_slope * mask * (1.0 - mask)
    descent[...] = gradient
    square_line = jnp.sum(gradient * gradient, axis=0, keepdims=True)
    which = lax.broadcasted_iota(jnp.int32, partial.shape, 0)
    sums = jnp.where(which == 0, loss_line, jnp.where(which == 1, square_line, 0.0))
    partial[...] = sums
    slots[me] = sums

    def share(step):
        return pltpu.make_async_remote_copy(
            src_ref=partial,
            dst_ref=slots.at[me],
            send_sem=sum_send.at[step],
            recv_sem=sum_recv.at[me],
            device_id=device(lax.rem(me + step, group)),
            device_id_type=MESH,
        )

    def arrival(step):
        source = lax.rem(me + step, group)
        return pltpu.make_async_remote_copy(
            src_ref=partial,
            dst_ref=slots.at[source],
            send_sem=sum_send.at[step],
            recv_sem=sum_recv.at[source],
            device_id=device(source),
            device_id_type=MESH,
        )

    def send_sums(step, carry):
        share(step).start()
        return carry

    def wait_sums(step, carry):
        arrival(step).wait()
        return carry

    lax.fori_loop(1, group, send_sums, 0)
    lax.fori_loop(1, group, wait_sums, 0)

    total = jnp.sum(slots[...], axis=0)
    pixels = rows * width * strips * cols
    loss_ref[0] = jnp.sum(total[0:1, :]) / (expos * pixels)
    square_sum = jnp.sum(total[1:2, :], axis=1, keepdims=True)
    root_mean = jnp.sqrt(square_sum / (expos * pixels) + norm_eps)
    new_ref[0] = params_ref[0] - step_length * descent[...] / root_mean


def tap_lines(col_taps, row_taps, length):
    kernels, parts, taps = col_taps.shape
    col, row = (col_taps.astype(F32), row_taps.astype(F32))
    gap = jnp.zeros((kernels, parts, length - taps), F32)
    wrap = jnp.concatenate([col[..., :1], gap, col[..., :0:-1]], axis=-1)
    ahead = jnp.concatenate([row, gap], axis=-1)
    turned = jnp.concatenate([row[..., ::-1], gap], axis=-1)
    return jnp.concatenate([wrap, ahead, turned, jnp.zeros_like(wrap)], axis=1)


def shards(mask_params, target, col_taps, row_taps, kernel_weights):
    rows, width = target.shape
    kernels, _, taps = col_taps.shape
    half = taps // 2
    two = 2 * half
    wide, tall = (width + 2 * two, rows + two)
    strips, cols, expos = (lax.axis_size(a) for a in ("strip", "col", "expo"))
    group = strips * cols * expos
    span = WINDOW - two
    vmem = pl.BlockSpec(memory_space=pltpu.VMEM)
    smem = pl.BlockSpec(memory_space=pltpu.SMEM)
    dma = pltpu.SemaphoreType.DMA
    return pl.pallas_call(
        functools.partial(body, (strips, cols, expos, half)),
        out_shape=(
            jax.ShapeDtypeStruct(mask_params.shape, F32),
            jax.ShapeDtypeStruct(target.shape, F32),
            jax.ShapeDtypeStruct((1,), F32),
        ),
        in_specs=[vmem, vmem, vmem, smem],
        out_specs=(vmem, vmem, smem),
        scratch_shapes=[
            pltpu.VMEM((2, rows + 2 * two, 3 * width), BF16),
            pltpu.VMEM((rows + 2 * two, wide), BF16),
            pltpu.VMEM((kernels, 2, wide, wide), BF16),
            pltpu.VMEM((kernels, 2, span, 2 * WINDOW), BF16),
            pltpu.VMEM((kernels, 2, span, 2 * WINDOW), BF16),
            pltpu.VMEM((2, rows + 2 * two, wide), BF16),
            pltpu.VMEM((kernels, 2, tall, wide), F32),
            pltpu.VMEM((tall, wide), F32),
            pltpu.VMEM((tall, wide), F32),
            pltpu.VMEM((tall, wide), F32),
            pltpu.VMEM((rows, width), F32),
            pltpu.VMEM((8, width), F32),
            pltpu.VMEM((group, 8, width), F32),
            dma((8,)),
            dma((8,)),
            dma,
            dma,
            dma((group,)),
            dma((group,)),
        ],
        compiler_params=pltpu.CompilerParams(
            collective_id=0, has_side_effects=True, vmem_limit_bytes=56 * 1024 * 1024
        ),
    )(mask_params, target, tap_lines(col_taps, row_taps, wide), kernel_weights)


def solution(mesh):
    return jax.shard_map(
        shards,
        mesh=mesh,
        in_specs=(
            P("expo", ("tiles", "strip"), "col"),
            P(("tiles", "strip"), "col"),
            P(),
            P(),
            P(),
        ),
        out_specs=(P("expo", ("tiles", "strip"), "col"), P(("tiles", "strip"), "col"), P("tiles")),
        check_vma=False,
    )
```

```python
import functools

import jax
import jax.numpy as jnp
from jax import lax
from jax.experimental import pallas as pl
from jax.experimental.pallas import tpu as pltpu
from jax.sharding import PartitionSpec as P

mask_slope = 4.0
resist_steep = 4.0
resist_level = 3.0
step_length = 0.5
norm_eps = 1e-06

MESH = pl.DeviceIdType.MESH
F32 = jnp.float32
BF16 = jnp.bfloat16
WINDOW = 256
DIRECTIONS = [(a, b) for a in (-1, 0, 1) for b in (-1, 0, 1) if (a, b) != (0, 0)]


def blocks_of(total_out, reach):
    most = WINDOW - reach
    count = -(-total_out // most)
    size = -(-total_out // (count * 16)) * 16
    found = []
    for start in range(0, total_out, size):
        rows = min(size, total_out - start)
        window = min(start, total_out + reach - WINDOW)
        found.append((start, rows, window, start - window))
    return found


def dot(a, b):
    return jnp.dot(a, b, preferred_element_type=F32)


def dot_t(a, b):
    return lax.dot_general(a, b, (((1,), (1,)), ((), ())), preferred_element_type=F32)


def body(
    sizes,
    params_ref,
    target_ref,
    col_ref,
    row_ref,
    weight_ref,
    new_ref,
    resist_ref,
    loss_ref,
    halo,
    ext,
    col_mats,
    fwd_mats,
    adj_mats,
    padded,
    lines,
    even,
    odd,
    fields,
    intensity,
    other,
    slope,
    descent,
    partial,
    slots,
    halo_send,
    halo_recv,
    expo_send,
    expo_recv,
    sum_send,
    sum_recv,
):
    strips, cols, expos, half = sizes
    kernels, parts, taps = col_ref.shape
    rows, width = target_ref.shape
    two = 2 * half
    wide = width + 2 * two
    group = strips * cols * expos
    strip, col, expo = (lax.axis_index("strip"), lax.axis_index("col"), lax.axis_index("expo"))
    me = (strip * cols + col) * expos + expo

    def device(index):
        return {
            "strip": index // (cols * expos),
            "col": (index // expos) % cols,
            "expo": index % expos,
        }

    halo[...] = jnp.zeros_like(halo)

    barrier = pltpu.get_barrier_semaphore()

    def greet(step, carry):
        pl.semaphore_signal(
            barrier, inc=1, device_id=device(lax.rem(me + step, group)), device_id_type=MESH
        )
        return carry

    lax.fori_loop(1, group, greet, 0)

    mask = jax.nn.sigmoid(mask_slope * params_ref[0])
    halo[0, two : two + rows, width : 2 * width] = mask.astype(BF16)
    halo[1, two : two + rows, width : 2 * width] = target_ref[...].astype(F32).astype(BF16)

    def transfer(number):
        down, right = DIRECTIONS[number]
        source = {-1: (two, two), 0: (two, rows), 1: (rows, two)}[down]
        landing = {-1: two + rows, 0: two, 1: 0}[down]
        lane = {-1: 2 * width, 0: width, 1: 0}[right]
        return pltpu.make_async_remote_copy(
            src_ref=halo.at[:, pl.ds(source[0], source[1]), pl.ds(width, width)],
            dst_ref=halo.at[:, pl.ds(landing, source[1]), pl.ds(lane, width)],
            send_sem=halo_send.at[number],
            recv_sem=halo_recv.at[number],
            device_id={
                "strip": jnp.clip(strip + down, 0, strips - 1),
                "col": jnp.clip(col + right, 0, cols - 1),
            },
            device_id_type=MESH,
        )

    def inside(down, right):
        to_strip, to_col = (strip + down, col + right)
        return (to_strip >= 0) & (to_strip < strips) & (to_col >= 0) & (to_col < cols)

    padded[...] = jnp.zeros_like(padded)
    for k in range(kernels):
        for table, source in enumerate((col_ref, row_ref)):
            padded[table, parts * k : parts * (k + 1), :taps] = source[k].astype(F32)
    tap_ids = lax.broadcasted_iota(jnp.int32, (padded.shape[2], wide), 0)
    places = lax.broadcasted_iota(jnp.int32, (padded.shape[2], wide), 1)

    def chosen(flags):
        return jnp.where(flags, 1.0, 0.0).astype(BF16)

    col_lines, row_lines = (padded[0].astype(BF16), padded[1].astype(BF16))
    lines[0] = dot(col_lines, chosen((tap_ids + places == wide) | (tap_ids + places == 0)))
    lines[1] = dot(row_lines, chosen(tap_ids == places))
    lines[2] = dot(row_lines, chosen(tap_ids + places == taps - 1))

    reach = wide // 2

    def circulant(table, k, part):
        line = lines[table, pl.ds(parts * k + part, 1), :]
        upper = pltpu.roll(
            jnp.broadcast_to(line, (reach, wide)), 0, 1, stride=1, stride_axis=0
        ).astype(BF16)
        lower = jnp.concatenate([upper[:, reach:], upper[:, :reach]], axis=1)
        return jnp.concatenate([upper, lower], axis=0)

    span = adj_mats.shape[2]
    groups = fwd_mats.shape[1]

    def build_cols(k, carry):
        for part in range(parts):
            col_mats[k, part] = circulant(0, k, part)
        return carry

    def build_rows(k, carry):
        t0, t1 = (circulant(1, k, part)[:span].reshape(groups, 16, wide) for part in range(2))
        fwd_mats[k, :, 0, :, :WINDOW] = t0
        fwd_mats[k, :, 0, :, WINDOW:] = -t1
        fwd_mats[k, :, 1, :, :WINDOW] = t1
        fwd_mats[k, :, 1, :, WINDOW:] = t0
        g0, g1 = (circulant(2, k, part)[:span] for part in range(2))
        adj_mats[k, 0, :, :WINDOW] = g0
        adj_mats[k, 0, :, WINDOW:] = g1
        adj_mats[k, 1, :, :WINDOW] = -g1
        adj_mats[k, 1, :, WINDOW:] = g0
        return carry

    lax.fori_loop(0, kernels, build_cols, 0)

    pl.semaphore_wait(barrier, group - 1)

    for number, (down, right) in enumerate(DIRECTIONS):

        @pl.when(inside(down, right))
        def _():
            transfer(number).start()

    lax.fori_loop(0, kernels, build_rows, 0)
    intensity[...] = jnp.zeros_like(intensity)
    descent[...] = jnp.zeros_like(descent)

    for number, (down, right) in enumerate(DIRECTIONS):

        @pl.when(inside(down, right))
        def _():
            transfer(number).wait_send()

        @pl.when(inside(-down, -right))
        def _():
            transfer(number).wait_recv()

    lanes = halo.shape[2]
    shifted = pltpu.roll(halo[0].astype(F32), lanes - (width - two), 1)
    ext[...] = shifted[:, :wide].astype(BF16)

    def fill(k, held):
        for part in range(parts):
            held[part] = dot(ext[...], col_mats[k, part]).astype(BF16)

    def use(k, held):
        weight = weight_ref[k]
        for start, count, window, offset in blocks_of(rows + two, two):
            source = jnp.concatenate(
                [held[part, window : window + WINDOW, :] for part in range(parts)], axis=0
            )
            picked = fwd_mats[k, offset // 16 : (offset + count) // 16]
            pair = dot(picked.reshape(2 * count, 2 * WINDOW), source)
            pair = pair.reshape(count // 16, 2, 16, wide)
            real_part = pair[:, 0].reshape(count, wide)
            imag_part = pair[:, 1].reshape(count, wide)
            fields[k, 0, start : start + count, :] = real_part.astype(BF16)
            fields[k, 1, start : start + count, :] = imag_part.astype(BF16)
            intensity[start : start + count, :] += weight * (
                real_part * real_part + imag_part * imag_part
            )

    def in_pairs(make, take):
        make(0, even)

        def step(j, carry):
            make(2 * j + 1, odd)
            take(2 * j, even)
            make(jnp.minimum(2 * j + 2, kernels - 1), even)
            take(2 * j + 1, odd)
            return carry

        lax.fori_loop(0, kernels // 2, step, 0)
        if kernels % 2:
            take(kernels - 1, even)

    in_pairs(fill, use)

    swap = pltpu.make_async_remote_copy(
        src_ref=intensity,
        dst_ref=other,
        send_sem=expo_send,
        recv_sem=expo_recv,
        device_id={"expo": 1 - expo},
        device_id_type=MESH,
    )
    swap.start()
    swap.wait()

    tall = rows + two
    resist = jax.nn.sigmoid(resist_steep * (intensity[...] + other[...] - resist_level))
    target_ext = pltpu.roll(
        halo[1, half : half + tall, :].astype(F32), lanes - (width - half), 1
    )[:, :wide]
    row_ids = lax.broadcasted_iota(jnp.int32, (tall, wide), 0) + (strip * rows - half)
    lane_ids = lax.broadcasted_iota(jnp.int32, (tall, wide), 1)
    col_ids = lane_ids + (col * width - half)
    kept = (
        (row_ids >= 0)
        & (row_ids < strips * rows)
        & (col_ids >= 0)
        & (col_ids < cols * width)
        & (lane_ids < width + two)
    )
    mismatch = resist - target_ext
    slope[...] = jnp.where(kept, 2.0 * mismatch * resist_steep * resist * (1.0 - resist), 0.0)
    own = pltpu.roll(resist[half : half + rows, :], wide - half, 1)[:, :width]
    resist_ref[...] = own
    own_miss = own - target_ref[...].astype(F32)
    loss_line = jnp.sum(own_miss * own_miss, axis=0, keepdims=True)

    def correlate(k, held):
        weighting = ((2.0 * weight_ref[k]) * slope[...]).astype(BF16)
        products = [weighting * fields[k, part] for part in range(parts)]
        for start, count, window, offset in blocks_of(rows, two):
            source = jnp.concatenate(
                [products[part][window : window + WINDOW, :] for part in range(parts)], axis=0
            )
            picked = jnp.concatenate(
                [adj_mats[k, part, offset : offset + count, :] for part in range(parts)], axis=0
            )
            returned = dot(picked, source).astype(BF16)
            for part in range(parts):
                held[part, start : start + count, :] = returned[part * count : (part + 1) * count]

    def gather(k, held):
        taps_now = jnp.concatenate(
            [col_mats[k, part, two : two + width, :] for part in range(parts)], axis=1
        )
        returned = jnp.concatenate([held[part, :rows, :] for part in range(parts)], axis=1)
        descent[...] += dot_t(returned, taps_now)

    in_pairs(correlate, gather)

    mask = jax.nn.sigmoid(mask_slope * params_ref[0])
    gradient = descent[...] * mask_slope * mask * (1.0 - mask)
    descent[...] = gradient
    square_line = jnp.sum(gradient * gradient, axis=0, keepdims=True)
    which = lax.broadcasted_iota(jnp.int32, partial.shape, 0)
    sums = jnp.where(which == 0, loss_line, jnp.where(which == 1, square_line, 0.0))
    partial[...] = sums
    slots[me] = sums

    def share(step):
        return pltpu.make_async_remote_copy(
            src_ref=partial,
            dst_ref=slots.at[me],
            send_sem=sum_send.at[step],
            recv_sem=sum_recv.at[me],
            device_id=device(lax.rem(me + step, group)),
            device_id_type=MESH,
        )

    def arrival(step):
        source = lax.rem(me + step, group)
        return pltpu.make_async_remote_copy(
            src_ref=partial,
            dst_ref=slots.at[source],
            send_sem=sum_send.at[step],
            recv_sem=sum_recv.at[source],
            device_id=device(source),
            device_id_type=MESH,
        )

    def send_sums(step, carry):
        share(step).start()
        return carry

    def wait_sums(step, carry):
        arrival(step).wait()
        return carry

    lax.fori_loop(1, group, send_sums, 0)
    lax.fori_loop(1, group, wait_sums, 0)

    total = jnp.sum(slots[...], axis=0)
    pixels = rows * width * strips * cols
    loss_ref[0] = jnp.sum(total[0:1, :]) / (expos * pixels)
    square_sum = jnp.sum(total[1:2, :], axis=1, keepdims=True)
    root_mean = jnp.sqrt(square_sum / (expos * pixels) + norm_eps)
    new_ref[0] = params_ref[0] - step_length * descent[...] / root_mean


def shards(mask_params, target, col_taps, row_taps, kernel_weights):
    rows, width = target.shape
    kernels, _, taps = col_taps.shape
    half = taps // 2
    two = 2 * half
    wide, tall = (width + 2 * two, rows + two)
    strips, cols, expos = (lax.axis_size(a) for a in ("strip", "col", "expo"))
    group = strips * cols * expos
    span = WINDOW - two
    vmem = pl.BlockSpec(memory_space=pltpu.VMEM)
    smem = pl.BlockSpec(memory_space=pltpu.SMEM)
    dma = pltpu.SemaphoreType.DMA
    return pl.pallas_call(
        functools.partial(body, (strips, cols, expos, half)),
        out_shape=(
            jax.ShapeDtypeStruct(mask_params.shape, F32),
            jax.ShapeDtypeStruct(target.shape, F32),
            jax.ShapeDtypeStruct((1,), F32),
        ),
        in_specs=[vmem, vmem, vmem, vmem, smem],
        out_specs=(vmem, vmem, smem),
        scratch_shapes=[
            pltpu.VMEM((2, rows + 2 * two, 3 * width), BF16),
            pltpu.VMEM((rows + 2 * two, wide), BF16),
            pltpu.VMEM((kernels, 2, wide, wide), BF16),
            pltpu.VMEM((kernels, span // 16, 2, 16, 2 * WINDOW), BF16),
            pltpu.VMEM((kernels, 2, span, 2 * WINDOW), BF16),
            pltpu.VMEM((2, 2 * kernels, wide // 2), F32),
            pltpu.VMEM((3, 2 * kernels, wide), F32),
            pltpu.VMEM((2, rows + 2 * two, wide), BF16),
            pltpu.VMEM((2, rows + 2 * two, wide), BF16),
            pltpu.VMEM((kernels, 2, tall, wide), BF16),
            pltpu.VMEM((tall, wide), F32),
            pltpu.VMEM((tall, wide), F32),
            pltpu.VMEM((tall, wide), F32),
            pltpu.VMEM((rows, width), F32),
            pltpu.VMEM((8, width), F32),
            pltpu.VMEM((group, 8, width), F32),
            dma((8,)),
            dma((8,)),
            dma,
            dma,
            dma((group,)),
            dma((group,)),
        ],
        compiler_params=pltpu.CompilerParams(
            collective_id=0, has_side_effects=True, vmem_limit_bytes=56 * 1024 * 1024
        ),
    )(mask_params, target, col_taps, row_taps, kernel_weights)


def solution(mesh):
    return jax.shard_map(
        shards,
        mesh=mesh,
        in_specs=(
            P("expo", ("tiles", "strip"), "col"),
            P(("tiles", "strip"), "col"),
            P(),
            P(),
            P(),
        ),
        out_specs=(P("expo", ("tiles", "strip"), "col"), P(("tiles", "strip"), "col"), P("tiles")),
        check_vma=False,
    )
```

```python
import functools

import jax
import jax.numpy as jnp
from jax import lax
from jax.experimental import pallas as pl
from jax.experimental.pallas import tpu as pltpu
from jax.sharding import PartitionSpec as P

mask_slope = 4.0
resist_steep = 4.0
resist_level = 3.0
step_length = 0.5
norm_eps = 1e-06

MESH = pl.DeviceIdType.MESH
F32 = jnp.float32
BF16 = jnp.bfloat16
DIRECTIONS = [(a, b) for a in (-1, 0, 1) for b in (-1, 0, 1) if (a, b) != (0, 0)]


def dot(a, b):
    return jnp.dot(a, b, preferred_element_type=F32)


def body(
    sizes,
    params_ref,
    target_ref,
    col_ref,
    row_ref,
    weight_ref,
    new_ref,
    resist_ref,
    loss_ref,
    halo,
    windows,
    padded,
    lines,
    col_mats,
    row_mats,
    row_adjoints,
    col_adjoints,
    columns,
    fields,
    intensity,
    other,
    slope,
    even,
    odd,
    descent,
    steps_ref,
    partial,
    slots,
    halo_send,
    halo_recv,
    expo_send,
    expo_recv,
    sum_send,
    sum_recv,
):
    strips, cols, expos, half = sizes
    kernels, parts, taps = col_ref.shape
    rows, width = target_ref.shape
    two = 2 * half
    tile = 2 * two
    wide = width + two
    bands = rows // tile
    group = strips * cols * expos
    strip, col, expo = (lax.axis_index("strip"), lax.axis_index("col"), lax.axis_index("expo"))
    me = (strip * cols + col) * expos + expo

    def device(index):
        return {
            "strip": index // (cols * expos),
            "col": (index // expos) % cols,
            "expo": index % expos,
        }

    halo[...] = jnp.zeros_like(halo)

    barrier = pltpu.get_barrier_semaphore()

    def greet(step, carry):
        pl.semaphore_signal(
            barrier, inc=1, device_id=device(lax.rem(me + step, group)), device_id_type=MESH
        )
        return carry

    lax.fori_loop(1, group, greet, 0)

    mask = jax.nn.sigmoid(mask_slope * params_ref[0])
    halo[0, two : two + width, tile : tile + rows] = mask.T.astype(BF16)
    target_now = target_ref[...].astype(F32)
    halo[1, two : two + width, tile : tile + rows] = target_now.T.astype(BF16)

    def transfer(number):
        down, right = DIRECTIONS[number]
        lane, lanes, to_lane = {
            -1: (tile, tile, tile + rows),
            0: (tile, rows, tile),
            1: (rows, tile, 0),
        }[down]
        place, places, to_place = {
            -1: (two, two, two + width),
            0: (two, width, two),
            1: (width, two, 0),
        }[right]
        return pltpu.make_async_remote_copy(
            src_ref=halo.at[:, pl.ds(place, places), pl.ds(lane, lanes)],
            dst_ref=halo.at[:, pl.ds(to_place, places), pl.ds(to_lane, lanes)],
            send_sem=halo_send.at[number],
            recv_sem=halo_recv.at[number],
            device_id={
                "strip": jnp.clip(strip + down, 0, strips - 1),
                "col": jnp.clip(col + right, 0, cols - 1),
            },
            device_id_type=MESH,
        )

    def inside(down, right):
        to_strip, to_col = (strip + down, col + right)
        return (to_strip >= 0) & (to_strip < strips) & (to_col >= 0) & (to_col < cols)

    padded[...] = jnp.zeros_like(padded)
    for k in range(kernels):
        for table, source in enumerate((col_ref, row_ref)):
            padded[table, parts * k : parts * (k + 1), :taps] = source[k].astype(F32)
    tap_ids = lax.broadcasted_iota(jnp.int32, (tile, tile), 0)
    places = lax.broadcasted_iota(jnp.int32, (tile, tile), 1)

    def chosen(flags):
        return jnp.where(flags, 1.0, 0.0).astype(BF16)

    col_lines, row_lines = (padded[0].astype(BF16), padded[1].astype(BF16))
    last = taps - 1
    lines[0] = dot(row_lines, chosen((tap_ids + places == tile) | (tap_ids + places == 0)))
    lines[1] = dot(
        row_lines, chosen((places - tap_ids == tile - last) | (tap_ids - places == last))
    )
    lines[2] = dot(col_lines, chosen(tap_ids + places == last))
    lower = tap_ids >= places
    upper = tap_ids <= places

    def rolled(line, count):
        return pltpu.roll(
            jnp.broadcast_to(line, (count, tile)), 0, 1, stride=1, stride_axis=0
        )

    def circulant(table, k, part):
        return rolled(lines[table, pl.ds(parts * k + part, 1), :], tile)

    def build_cols(k, carry):
        for part in range(parts):
            line = padded[0, pl.ds(parts * k + part, 1), :]
            col_mats[k, part * two : (part + 1) * two, :] = rolled(line, two).astype(BF16)
        return carry

    def build_rows(k, carry):
        t0, t1 = (circulant(0, k, part) for part in range(parts))
        for half_id, keep in enumerate((lower, ~lower)):
            a0, a1 = (jnp.where(keep, t, 0.0).astype(BF16) for t in (t0, t1))
            top = 2 * tile * half_id
            row_mats[k, top : top + tile, :tile] = a0
            row_mats[k, top : top + tile, tile:] = a1
            row_mats[k, top + tile : top + 2 * tile, :tile] = -a1
            row_mats[k, top + tile : top + 2 * tile, tile:] = a0
        return carry

    def build_adjoints(k, carry):
        t0, t1 = (circulant(1, k, part) for part in range(parts))
        for half_id, keep in enumerate((lower, ~lower)):
            a0, a1 = (jnp.where(keep, t, 0.0).astype(BF16) for t in (t0, t1))
            top = 2 * tile * half_id
            row_adjoints[k, top : top + tile, :tile] = a0
            row_adjoints[k, top : top + tile, tile:] = -a1
            row_adjoints[k, top + tile : top + 2 * tile, :tile] = a1
            row_adjoints[k, top + tile : top + 2 * tile, tile:] = a0
        u0, u1 = (circulant(2, k, part) for part in range(parts))
        col_adjoints[k, :, :tile] = jnp.where(upper, u0, 0.0).astype(BF16)
        col_adjoints[k, :, tile : 2 * tile] = jnp.where(upper, u1, 0.0).astype(BF16)
        r0 = jnp.where(upper, 0.0, u0)
        r1 = pltpu.roll(jnp.where(upper, 0.0, u1), two, 1)
        col_adjoints[k, :, 2 * tile :] = jnp.where(places < two, r0, r1).astype(BF16)
        return carry

    lax.fori_loop(0, kernels, build_cols, 0)

    pl.semaphore_wait(barrier, group - 1)

    for number, (down, right) in enumerate(DIRECTIONS):

        @pl.when(inside(down, right))
        def _():
            transfer(number).start()

    lax.fori_loop(0, kernels, build_rows, 0)
    intensity[...] = jnp.zeros_like(intensity)
    descent[...] = jnp.zeros_like(descent)

    for number, (down, right) in enumerate(DIRECTIONS):

        @pl.when(inside(down, right))
        def _():
            transfer(number).wait_send()

        @pl.when(inside(-down, -right))
        def _():
            transfer(number).wait_recv()

    lanes = halo.shape[2]
    reach = rows + tile
    shifted = pltpu.roll(halo[0].astype(F32), lanes - two, 1)[:, :reach].astype(BF16)
    steps = wide // two
    for step in range(steps):
        windows[:, step * reach : (step + 1) * reach] = shifted[step * two : step * two + tile]

    batch = next(size for size in (4, 3, 2, 1) if kernels % size == 0)

    def col_pass(j, carry):
        first = j * batch
        made = dot(
            col_mats[pl.ds(first, batch)].reshape(batch * parts * two, tile), windows[...]
        ).astype(BF16)
        for i in range(batch):
            for part in range(parts):
                top = (i * parts + part) * two
                for step in range(steps):
                    for band in range(bands + 1):
                        lane = step * reach + band * tile
                        columns[
                            first + i,
                            band,
                            step * two : (step + 1) * two,
                            part * tile : (part + 1) * tile,
                        ] = made[top : top + two, lane : lane + tile]
        return carry

    lax.fori_loop(0, kernels // batch, col_pass, 0)

    def row_pass(k):
        weight = weight_ref[k]
        held = [columns[k, band] for band in range(bands + 1)]
        joined = jnp.concatenate(
            [jnp.concatenate(held[band : band + 2], axis=1) for band in range(bands)], axis=0
        )
        whole = dot(joined, row_mats[k])
        tail = dot(held[bands], row_mats[k, : 2 * tile, :])
        for band in range(bands + 1):
            pair = tail if band == bands else whole[band * wide : (band + 1) * wide]
            fields[k, band] = pair.astype(BF16)
            real_part, imag_part = (pair[:, :tile], pair[:, tile:])
            intensity[band] += weight * (real_part * real_part + imag_part * imag_part)

    unroll = next(size for size in (2, 1) if kernels % size == 0)

    def row_passes(j, carry):
        for i in range(unroll):
            row_pass(j * unroll + i)
        return carry

    lax.fori_loop(0, kernels // unroll, row_passes, 0)

    def in_pairs(make, take):
        make(0, even)

        def step(j, carry):
            make(2 * j + 1, odd)
            take(2 * j, even)
            make(jnp.minimum(2 * j + 2, kernels - 1), even)
            take(2 * j + 1, odd)
            return carry

        lax.fori_loop(0, kernels // 2, step, 0)
        if kernels % 2:
            take(kernels - 1, even)

    swap = pltpu.make_async_remote_copy(
        src_ref=intensity,
        dst_ref=other,
        send_sem=expo_send,
        recv_sem=expo_recv,
        device_id={"expo": 1 - expo},
        device_id_type=MESH,
    )
    swap.start()
    lax.fori_loop(0, kernels, build_adjoints, 0)
    swap.wait()

    def side_by_side(ref):
        return jnp.concatenate([ref[band] for band in range(bands + 1)], axis=1)

    total = side_by_side(intensity) + side_by_side(other)
    resist = jax.nn.sigmoid(resist_steep * (total - resist_level))
    target_ext = pltpu.roll(
        halo[1, half : half + wide, :].astype(F32), lanes - (tile - half), 1
    )[:, :reach]
    row_lanes = lax.broadcasted_iota(jnp.int32, (wide, reach), 1)
    row_ids = row_lanes + (strip * rows - half)
    col_ids = lax.broadcasted_iota(jnp.int32, (wide, reach), 0) + (col * width - half)
    kept = (
        (row_ids >= 0)
        & (row_ids < strips * rows)
        & (col_ids >= 0)
        & (col_ids < cols * width)
        & (row_lanes < rows + two)
    )
    mismatch = resist - target_ext
    steepness = jnp.where(kept, 2.0 * mismatch * resist_steep * resist * (1.0 - resist), 0.0)
    for band in range(bands + 1):
        slope[band] = steepness[:, band * tile : (band + 1) * tile]
    own = pltpu.roll(resist[half : half + width, :], reach - half, 1)[:, :rows].T
    resist_ref[...] = own
    own_miss = own - target_ref[...].astype(F32)
    loss_line = jnp.sum(own_miss * own_miss, axis=0, keepdims=True)

    def correlate(k, held):
        scale = 2.0 * weight_ref[k]
        products = []
        for band in range(bands + 1):
            weighting = (scale * slope[band]).astype(BF16)
            products.append(fields[k, band] * jnp.concatenate([weighting] * parts, axis=1))
        joined = jnp.concatenate(
            [jnp.concatenate(products[band : band + 2], axis=1) for band in range(bands)], axis=0
        )
        returned = dot(joined, row_adjoints[k]).astype(BF16)
        for band in range(bands):
            held[band] = returned[band * wide : (band + 1) * wide]

    def gather(k, held):
        found = [
            jnp.concatenate(
                [held[band, :, part * tile : (part + 1) * tile] for band in range(bands)], axis=1
            )
            for part in range(parts)
        ]
        source = jnp.concatenate([f[:tile] for f in found] + [f[tile:] for f in found], axis=0)
        descent[...] += dot(col_adjoints[k], source)

    in_pairs(correlate, gather)

    mask = jax.nn.sigmoid(mask_slope * params_ref[0])
    gradient = descent[...].T * mask_slope * mask * (1.0 - mask)
    steps_ref[...] = gradient
    square_line = jnp.sum(gradient * gradient, axis=0, keepdims=True)
    which = lax.broadcasted_iota(jnp.int32, partial.shape, 0)
    sums = jnp.where(which == 0, loss_line, jnp.where(which == 1, square_line, 0.0))
    partial[...] = sums
    slots[me] = sums

    def share(step):
        return pltpu.make_async_remote_copy(
            src_ref=partial,
            dst_ref=slots.at[me],
            send_sem=sum_send.at[step],
            recv_sem=sum_recv.at[me],
            device_id=device(lax.rem(me + step, group)),
            device_id_type=MESH,
        )

    def arrival(step):
        source = lax.rem(me + step, group)
        return pltpu.make_async_remote_copy(
            src_ref=partial,
            dst_ref=slots.at[source],
            send_sem=sum_send.at[step],
            recv_sem=sum_recv.at[source],
            device_id=device(source),
            device_id_type=MESH,
        )

    def send_sums(step, carry):
        share(step).start()
        return carry

    def wait_sums(step, carry):
        arrival(step).wait()
        return carry

    lax.fori_loop(1, group, send_sums, 0)
    lax.fori_loop(1, group, wait_sums, 0)

    totals = jnp.sum(slots[...], axis=0)
    pixels = rows * width * strips * cols
    loss_ref[0] = jnp.sum(totals[0:1, :]) / (expos * pixels)
    square_sum = jnp.sum(totals[1:2, :], axis=1, keepdims=True)
    root_mean = jnp.sqrt(square_sum / (expos * pixels) + norm_eps)
    new_ref[0] = params_ref[0] - step_length * steps_ref[...] / root_mean


def shards(mask_params, target, col_taps, row_taps, kernel_weights):
    rows, width = target.shape
    kernels, _, taps = col_taps.shape
    half = taps // 2
    two = 2 * half
    tile, wide, bands = (2 * two, width + two, rows // (2 * two))
    strips, cols, expos = (lax.axis_size(a) for a in ("strip", "col", "expo"))
    group = strips * cols * expos
    vmem = pl.BlockSpec(memory_space=pltpu.VMEM)
    smem = pl.BlockSpec(memory_space=pltpu.SMEM)
    dma = pltpu.SemaphoreType.DMA
    return pl.pallas_call(
        functools.partial(body, (strips, cols, expos, half)),
        out_shape=(
            jax.ShapeDtypeStruct(mask_params.shape, F32),
            jax.ShapeDtypeStruct(target.shape, F32),
            jax.ShapeDtypeStruct((1,), F32),
        ),
        in_specs=[vmem, vmem, vmem, vmem, smem],
        out_specs=(vmem, vmem, smem),
        scratch_shapes=[
            pltpu.VMEM((2, width + 2 * two, rows + 2 * tile), BF16),
            pltpu.VMEM((tile, (wide // two) * (rows + tile)), BF16),
            pltpu.VMEM((2, 2 * kernels, tile), F32),
            pltpu.VMEM((3, 2 * kernels, tile), F32),
            pltpu.VMEM((kernels, 2 * two, tile), BF16),
            pltpu.VMEM((kernels, 4 * tile, 2 * tile), BF16),
            pltpu.VMEM((kernels, 4 * tile, 2 * tile), BF16),
            pltpu.VMEM((kernels, width, 3 * tile), BF16),
            pltpu.VMEM((kernels, bands + 1, wide, 2 * tile), BF16),
            pltpu.VMEM((kernels, bands + 1, wide, 2 * tile), BF16),
            pltpu.VMEM((bands + 1, wide, tile), F32),
            pltpu.VMEM((bands + 1, wide, tile), F32),
            pltpu.VMEM((bands + 1, wide, tile), F32),
            pltpu.VMEM((bands, wide, 2 * tile), BF16),
            pltpu.VMEM((bands, wide, 2 * tile), BF16),
            pltpu.VMEM((width, rows), F32),
            pltpu.VMEM((rows, width), F32),
            pltpu.VMEM((8, width), F32),
            pltpu.VMEM((group, 8, width), F32),
            dma((8,)),
            dma((8,)),
            dma,
            dma,
            dma((group,)),
            dma((group,)),
        ],
        compiler_params=pltpu.CompilerParams(
            collective_id=0, has_side_effects=True, vmem_limit_bytes=56 * 1024 * 1024
        ),
    )(mask_params, target, col_taps, row_taps, kernel_weights)


def solution(mesh):
    return jax.shard_map(
        shards,
        mesh=mesh,
        in_specs=(
            P("expo", ("tiles", "strip"), "col"),
            P(("tiles", "strip"), "col"),
            P(),
            P(),
            P(),
        ),
        out_specs=(P("expo", ("tiles", "strip"), "col"), P(("tiles", "strip"), "col"), P("tiles")),
        check_vma=False,
    )
```

```python
import functools

import jax
import jax.numpy as jnp
from jax import lax
from jax.experimental import pallas as pl
from jax.experimental.pallas import tpu as pltpu
from jax.sharding import PartitionSpec as P

mask_slope = 4.0
resist_steep = 4.0
resist_level = 3.0
step_length = 0.5
norm_eps = 1e-06

MESH = pl.DeviceIdType.MESH
F32 = jnp.float32
BF16 = jnp.bfloat16
DIRECTIONS = [(a, b) for a in (-1, 0, 1) for b in (-1, 0, 1) if (a, b) != (0, 0)]


def dot(a, b):
    return jnp.dot(a, b, preferred_element_type=F32)


def body(
    sizes,
    params_ref,
    target_ref,
    col_ref,
    row_ref,
    weight_ref,
    new_ref,
    resist_ref,
    loss_ref,
    halo,
    windows,
    padded,
    lines,
    masks,
    col_mats,
    row_mats,
    row_adjoints,
    col_adjoints,
    columns,
    fields,
    intensity,
    other,
    slope,
    even,
    odd,
    descent,
    steps_ref,
    partial,
    slots,
    halo_send,
    halo_recv,
    expo_send,
    expo_recv,
    sum_send,
    sum_recv,
):
    strips, cols, expos, half = sizes
    kernels, parts, taps = col_ref.shape
    rows, width = target_ref.shape
    two = 2 * half
    tile = 2 * two
    wide = width + two
    bands = rows // tile
    group = strips * cols * expos
    strip, col, expo = (lax.axis_index("strip"), lax.axis_index("col"), lax.axis_index("expo"))
    me = (strip * cols + col) * expos + expo

    def device(index):
        return {
            "strip": index // (cols * expos),
            "col": (index // expos) % cols,
            "expo": index % expos,
        }

    halo[...] = jnp.zeros_like(halo)

    barrier = pltpu.get_barrier_semaphore()

    def greet(step, carry):
        pl.semaphore_signal(
            barrier, inc=1, device_id=device(lax.rem(me + step, group)), device_id_type=MESH
        )
        return carry

    lax.fori_loop(1, group, greet, 0)

    mask = jax.nn.sigmoid(mask_slope * params_ref[0])
    halo[0, two : two + width, tile : tile + rows] = mask.T.astype(BF16)
    target_now = target_ref[...].astype(F32)
    halo[1, two : two + width, tile : tile + rows] = target_now.T.astype(BF16)

    def transfer(number):
        down, right = DIRECTIONS[number]
        lane, lanes, to_lane = {
            -1: (tile, tile, tile + rows),
            0: (tile, rows, tile),
            1: (rows, tile, 0),
        }[down]
        place, places, to_place = {
            -1: (two, two, two + width),
            0: (two, width, two),
            1: (width, two, 0),
        }[right]
        return pltpu.make_async_remote_copy(
            src_ref=halo.at[:, pl.ds(place, places), pl.ds(lane, lanes)],
            dst_ref=halo.at[:, pl.ds(to_place, places), pl.ds(to_lane, lanes)],
            send_sem=halo_send.at[number],
            recv_sem=halo_recv.at[number],
            device_id={
                "strip": jnp.clip(strip + down, 0, strips - 1),
                "col": jnp.clip(col + right, 0, cols - 1),
            },
            device_id_type=MESH,
        )

    def inside(down, right):
        to_strip, to_col = (strip + down, col + right)
        return (to_strip >= 0) & (to_strip < strips) & (to_col >= 0) & (to_col < cols)

    padded[...] = jnp.zeros_like(padded)
    for k in range(kernels):
        for table, source in enumerate((col_ref, row_ref)):
            padded[table, parts * k : parts * (k + 1), :taps] = source[k].astype(F32)
    tap_ids = lax.broadcasted_iota(jnp.int32, (tile, tile), 0)
    places = lax.broadcasted_iota(jnp.int32, (tile, tile), 1)

    def chosen(flags):
        return jnp.where(flags, 1.0, 0.0).astype(BF16)

    col_lines, row_lines = (padded[0].astype(BF16), padded[1].astype(BF16))
    last = taps - 1
    lines[0] = dot(row_lines, chosen((tap_ids + places == tile) | (tap_ids + places == 0)))
    lines[1] = dot(
        row_lines, chosen((places - tap_ids == tile - last) | (tap_ids - places == last))
    )
    lines[2] = dot(col_lines, chosen(tap_ids + places == last))
    masks[0] = chosen(tap_ids >= places)
    masks[1] = chosen(tap_ids < places)
    masks[2] = chosen(tap_ids <= places)
    masks[3] = chosen(tap_ids > jnp.where(places < two, places, places - two))

    def rolled(line, count):
        return pltpu.roll(
            jnp.broadcast_to(line, (count, tile)), 0, 1, stride=1, stride_axis=0
        )

    def circulant(table, k, part):
        return rolled(lines[table, pl.ds(parts * k + part, 1), :], tile)

    def build_cols(k, carry):
        for part in range(parts):
            line = padded[0, pl.ds(parts * k + part, 1), :]
            col_mats[k, part * two : (part + 1) * two, :] = rolled(line, two).astype(BF16)
        return carry

    def triangles(table, k, kept):
        t0, t1 = (circulant(table, k, part).astype(BF16) for part in range(parts))
        for side in range(2):
            a1 = t1 * masks[side]
            kept[k, side, 0] = t0 * masks[side]
            kept[k, side, 1] = a1
            kept[k, side, 2] = -a1

    def build_rows(k, carry):
        triangles(0, k, row_mats)
        return carry

    def build_adjoints(k):
        triangles(1, k, row_adjoints)
        u0, u1 = (circulant(2, k, part) for part in range(parts))
        col_adjoints[k, :, :tile] = u0.astype(BF16) * masks[2]
        col_adjoints[k, :, tile : 2 * tile] = u1.astype(BF16) * masks[2]
        mixed = jnp.where(places < two, u0, pltpu.roll(u1, two, 1)).astype(BF16)
        col_adjoints[k, :, 2 * tile :] = mixed * masks[3]

    def square(kept, k, side, top, bottom):
        plain = kept[k, side, 0]
        return jnp.concatenate(
            [
                jnp.concatenate([plain, kept[k, side, top]], axis=1),
                jnp.concatenate([kept[k, side, bottom], plain], axis=1),
            ],
            axis=0,
        )

    lax.fori_loop(0, kernels, build_cols, 0)

    pl.semaphore_wait(barrier, group - 1)

    for number, (down, right) in enumerate(DIRECTIONS):

        @pl.when(inside(down, right))
        def _():
            transfer(number).start()

    lax.fori_loop(0, kernels, build_rows, 0)
    intensity[...] = jnp.zeros_like(intensity)
    descent[...] = jnp.zeros_like(descent)

    for number, (down, right) in enumerate(DIRECTIONS):

        @pl.when(inside(down, right))
        def _():
            transfer(number).wait_send()

        @pl.when(inside(-down, -right))
        def _():
            transfer(number).wait_recv()

    lanes = halo.shape[2]
    reach = rows + tile
    shifted = pltpu.roll(halo[0].astype(F32), lanes - two, 1)[:, :reach].astype(BF16)
    steps = wide // two
    for step in range(steps):
        windows[:, step * reach : (step + 1) * reach] = shifted[step * two : step * two + tile]

    batch = next(size for size in (4, 3, 2, 1) if kernels % size == 0)

    def col_pass(j, carry):
        first = j * batch
        made = dot(
            col_mats[pl.ds(first, batch)].reshape(batch * parts * two, tile), windows[...]
        ).astype(BF16)
        for i in range(batch):
            for part in range(parts):
                top = (i * parts + part) * two
                for step in range(steps):
                    for band in range(bands + 1):
                        lane = step * reach + band * tile
                        columns[
                            first + i,
                            band,
                            step * two : (step + 1) * two,
                            part * tile : (part + 1) * tile,
                        ] = made[top : top + two, lane : lane + tile]
        return carry

    lax.fori_loop(0, kernels // batch, col_pass, 0)

    def row_pass(k):
        weight = weight_ref[k]
        held = [columns[k, band] for band in range(bands + 1)]
        joined = jnp.concatenate(
            [jnp.concatenate(held[band : band + 2], axis=1) for band in range(bands)], axis=0
        )
        first, second = (square(row_mats, k, side, 1, 2) for side in range(2))
        whole = dot(joined, jnp.concatenate([first, second], axis=0))
        tail = dot(held[bands], first)
        for band in range(bands + 1):
            pair = tail if band == bands else whole[band * wide : (band + 1) * wide]
            fields[k, band] = pair.astype(BF16)
            real_part, imag_part = (pair[:, :tile], pair[:, tile:])
            intensity[band] += weight * (real_part * real_part + imag_part * imag_part)

    unroll = next(size for size in (4, 3, 2, 1) if kernels % size == 0)

    def row_passes(j, carry):
        for i in range(unroll):
            row_pass(j * unroll + i)
            build_adjoints(j * unroll + i)
        return carry

    lax.fori_loop(0, kernels // unroll, row_passes, 0)

    def in_pairs(make, take):
        make(0, even)
        helds = (even, odd)
        size = next(size for size in (4, 2, 1) if kernels % size == 0)

        def step(j, carry):
            for i in range(size):
                k = size * j + i
                make(jnp.minimum(k + 1, kernels - 1), helds[(i + 1) % 2])
                take(k, helds[i % 2])
            return carry

        lax.fori_loop(0, kernels // size, step, 0)

    swap = pltpu.make_async_remote_copy(
        src_ref=intensity,
        dst_ref=other,
        send_sem=expo_send,
        recv_sem=expo_recv,
        device_id={"expo": 1 - expo},
        device_id_type=MESH,
    )
    swap.start()
    swap.wait()

    def side_by_side(ref):
        return jnp.concatenate([ref[band] for band in range(bands + 1)], axis=1)

    total = side_by_side(intensity) + side_by_side(other)
    resist = jax.nn.sigmoid(resist_steep * (total - resist_level))
    target_ext = pltpu.roll(
        halo[1, half : half + wide, :].astype(F32), lanes - (tile - half), 1
    )[:, :reach]
    row_lanes = lax.broadcasted_iota(jnp.int32, (wide, reach), 1)
    row_ids = row_lanes + (strip * rows - half)
    col_ids = lax.broadcasted_iota(jnp.int32, (wide, reach), 0) + (col * width - half)
    kept = (
        (row_ids >= 0)
        & (row_ids < strips * rows)
        & (col_ids >= 0)
        & (col_ids < cols * width)
        & (row_lanes < rows + two)
    )
    mismatch = resist - target_ext
    steepness = jnp.where(kept, 2.0 * mismatch * resist_steep * resist * (1.0 - resist), 0.0)
    for band in range(bands + 1):
        slope[band] = steepness[:, band * tile : (band + 1) * tile]
    own = pltpu.roll(resist[half : half + width, :], reach - half, 1)[:, :rows].T
    resist_ref[...] = own
    own_miss = own - target_ref[...].astype(F32)
    loss_line = jnp.sum(own_miss * own_miss, axis=0, keepdims=True)

    def correlate(k, held):
        scale = 2.0 * weight_ref[k]
        products = []
        for band in range(bands + 1):
            weighting = (scale * slope[band]).astype(BF16)
            products.append(fields[k, band] * jnp.concatenate([weighting] * parts, axis=1))
        joined = jnp.concatenate(
            [jnp.concatenate(products[band : band + 2], axis=1) for band in range(bands)], axis=0
        )
        matrix = jnp.concatenate(
            [square(row_adjoints, k, side, 2, 1) for side in range(2)], axis=0
        )
        returned = dot(joined, matrix).astype(BF16)
        for band in range(bands):
            held[band] = returned[band * wide : (band + 1) * wide]

    def gather(k, held):
        found = [
            jnp.concatenate(
                [held[band, :, part * tile : (part + 1) * tile] for band in range(bands)], axis=1
            )
            for part in range(parts)
        ]
        source = jnp.concatenate([f[:tile] for f in found] + [f[tile:] for f in found], axis=0)
        descent[...] += dot(col_adjoints[k], source)

    in_pairs(correlate, gather)

    mask = jax.nn.sigmoid(mask_slope * params_ref[0])
    gradient = descent[...].T * mask_slope * mask * (1.0 - mask)
    steps_ref[...] = gradient
    square_line = jnp.sum(gradient * gradient, axis=0, keepdims=True)
    which = lax.broadcasted_iota(jnp.int32, partial.shape, 0)
    sums = jnp.where(which == 0, loss_line, jnp.where(which == 1, square_line, 0.0))
    partial[...] = sums
    slots[me] = sums

    def share(step):
        return pltpu.make_async_remote_copy(
            src_ref=partial,
            dst_ref=slots.at[me],
            send_sem=sum_send.at[step],
            recv_sem=sum_recv.at[me],
            device_id=device(lax.rem(me + step, group)),
            device_id_type=MESH,
        )

    def arrival(step):
        source = lax.rem(me + step, group)
        return pltpu.make_async_remote_copy(
            src_ref=partial,
            dst_ref=slots.at[source],
            send_sem=sum_send.at[step],
            recv_sem=sum_recv.at[source],
            device_id=device(source),
            device_id_type=MESH,
        )

    def send_sums(step, carry):
        share(step).start()
        return carry

    def wait_sums(step, carry):
        arrival(step).wait()
        return carry

    lax.fori_loop(1, group, send_sums, 0)
    lax.fori_loop(1, group, wait_sums, 0)

    totals = jnp.sum(slots[...], axis=0)
    pixels = rows * width * strips * cols
    loss_ref[0] = jnp.sum(totals[0:1, :]) / (expos * pixels)
    square_sum = jnp.sum(totals[1:2, :], axis=1, keepdims=True)
    root_mean = jnp.sqrt(square_sum / (expos * pixels) + norm_eps)
    new_ref[0] = params_ref[0] - step_length * steps_ref[...] / root_mean


def shards(mask_params, target, col_taps, row_taps, kernel_weights):
    rows, width = target.shape
    kernels, _, taps = col_taps.shape
    half = taps // 2
    two = 2 * half
    tile, wide, bands = (2 * two, width + two, rows // (2 * two))
    strips, cols, expos = (lax.axis_size(a) for a in ("strip", "col", "expo"))
    group = strips * cols * expos
    vmem = pl.BlockSpec(memory_space=pltpu.VMEM)
    smem = pl.BlockSpec(memory_space=pltpu.SMEM)
    dma = pltpu.SemaphoreType.DMA
    return pl.pallas_call(
        functools.partial(body, (strips, cols, expos, half)),
        out_shape=(
            jax.ShapeDtypeStruct(mask_params.shape, F32),
            jax.ShapeDtypeStruct(target.shape, F32),
            jax.ShapeDtypeStruct((1,), F32),
        ),
        in_specs=[vmem, vmem, vmem, vmem, smem],
        out_specs=(vmem, vmem, smem),
        scratch_shapes=[
            pltpu.VMEM((2, width + 2 * two, rows + 2 * tile), BF16),
            pltpu.VMEM((tile, (wide // two) * (rows + tile)), BF16),
            pltpu.VMEM((2, 2 * kernels, tile), F32),
            pltpu.VMEM((3, 2 * kernels, tile), F32),
            pltpu.VMEM((4, tile, tile), BF16),
            pltpu.VMEM((kernels, 2 * two, tile), BF16),
            pltpu.VMEM((kernels, 2, 3, tile, tile), BF16),
            pltpu.VMEM((kernels, 2, 3, tile, tile), BF16),
            pltpu.VMEM((kernels, width, 3 * tile), BF16),
            pltpu.VMEM((kernels, bands + 1, wide, 2 * tile), BF16),
            pltpu.VMEM((kernels, bands + 1, wide, 2 * tile), BF16),
            pltpu.VMEM((bands + 1, wide, tile), F32),
            pltpu.VMEM((bands + 1, wide, tile), F32),
            pltpu.VMEM((bands + 1, wide, tile), F32),
            pltpu.VMEM((bands, wide, 2 * tile), BF16),
            pltpu.VMEM((bands, wide, 2 * tile), BF16),
            pltpu.VMEM((width, rows), F32),
            pltpu.VMEM((rows, width), F32),
            pltpu.VMEM((8, width), F32),
            pltpu.VMEM((group, 8, width), F32),
            dma((8,)),
            dma((8,)),
            dma,
            dma,
            dma((group,)),
            dma((group,)),
        ],
        compiler_params=pltpu.CompilerParams(
            collective_id=0, has_side_effects=True, vmem_limit_bytes=56 * 1024 * 1024
        ),
    )(mask_params, target, col_taps, row_taps, kernel_weights)


def solution(mesh):
    return jax.shard_map(
        shards,
        mesh=mesh,
        in_specs=(
            P("expo", ("tiles", "strip"), "col"),
            P(("tiles", "strip"), "col"),
            P(),
            P(),
            P(),
        ),
        out_specs=(P("expo", ("tiles", "strip"), "col"), P(("tiles", "strip"), "col"), P("tiles")),
        check_vma=False,
    )
```

```python
import functools

import jax
import jax.numpy as jnp
from jax import lax
from jax.experimental import pallas as pl
from jax.experimental.pallas import tpu as pltpu
from jax.sharding import PartitionSpec as P

mask_slope = 4.0
resist_steep = 4.0
resist_level = 3.0
step_length = 0.5
norm_eps = 1e-06

MESH = pl.DeviceIdType.MESH
F32 = jnp.float32
BF16 = jnp.bfloat16
DIRECTIONS = [(a, b) for a in (-1, 0, 1) for b in (-1, 0, 1) if (a, b) != (0, 0)]


def dot(a, b):
    return jnp.dot(a, b, preferred_element_type=F32)


def body(
    sizes,
    params_hbm,
    target_hbm,
    col_ref,
    row_ref,
    weight_ref,
    steps_ref,
    resist_ref,
    totals_ref,
    params_ref,
    target_ref,
    halo,
    windows,
    padded,
    lines,
    masks,
    col_mats,
    row_mats,
    row_adjoints,
    col_adjoints,
    even_columns,
    odd_columns,
    fields,
    intensity,
    other,
    slope,
    even,
    odd,
    descent,
    partial,
    slots,
    fetch_sem,
    halo_send,
    halo_recv,
    expo_send,
    expo_recv,
    sum_send,
    sum_recv,
):
    strips, cols, expos, half = sizes
    kernels, parts, taps = col_ref.shape
    rows, width = target_ref.shape
    two = 2 * half
    tile = 2 * two
    wide = width + two
    bands = rows // tile
    group = strips * cols * expos
    strip, col, expo = (lax.axis_index("strip"), lax.axis_index("col"), lax.axis_index("expo"))
    me = (strip * cols + col) * expos + expo

    def beyond(index, step, count):
        moved = index + step
        return jnp.where(moved >= count, moved - count, moved)

    peers = []
    for number in range(1, group):
        steps_to = (number // (cols * expos), number // expos % cols, number % expos)
        there = [
            beyond(index, step, count) if step else index
            for index, step, count in zip((strip, col, expo), steps_to, sizes[:3])
        ]
        peers.append(
            (
                dict(zip(("strip", "col", "expo"), there)),
                (there[0] * cols + there[1]) * expos + there[2],
            )
        )

    fetches = [
        pltpu.make_async_copy(source, into, fetch_sem.at[number])
        for number, (source, into) in enumerate(
            ((params_hbm, params_ref), (target_hbm, target_ref))
        )
    ]
    for fetch in fetches:
        fetch.start()

    halo[...] = jnp.zeros_like(halo)

    barrier = pltpu.get_barrier_semaphore()

    for place, _ in peers:
        pl.semaphore_signal(barrier, inc=1, device_id=place, device_id_type=MESH)

    for fetch in fetches:
        fetch.wait()
    mask = jax.nn.sigmoid(mask_slope * params_ref[0])
    halo[0, two : two + width, tile : tile + rows] = mask.T.astype(BF16)
    target_now = target_ref[...].astype(F32)
    halo[1, two : two + width, tile : tile + rows] = target_now.T.astype(BF16)

    def transfer(number):
        down, right = DIRECTIONS[number]
        lane, lanes, to_lane = {
            -1: (tile, tile, tile + rows),
            0: (tile, rows, tile),
            1: (rows, tile, 0),
        }[down]
        place, places, to_place = {
            -1: (two, two, two + width),
            0: (two, width, two),
            1: (width, two, 0),
        }[right]
        return pltpu.make_async_remote_copy(
            src_ref=halo.at[:, pl.ds(place, places), pl.ds(lane, lanes)],
            dst_ref=halo.at[:, pl.ds(to_place, places), pl.ds(to_lane, lanes)],
            send_sem=halo_send.at[number],
            recv_sem=halo_recv.at[number],
            device_id={
                "strip": jnp.clip(strip + down, 0, strips - 1),
                "col": jnp.clip(col + right, 0, cols - 1),
            },
            device_id_type=MESH,
        )

    def inside(down, right):
        to_strip, to_col = (strip + down, col + right)
        return (to_strip >= 0) & (to_strip < strips) & (to_col >= 0) & (to_col < cols)

    padded[...] = jnp.zeros_like(padded)
    for k in range(kernels):
        for table, source in enumerate((col_ref, row_ref)):
            padded[table, parts * k : parts * (k + 1), :taps] = source[k].astype(F32)
    tap_ids = lax.broadcasted_iota(jnp.int32, (tile, tile), 0)
    places = lax.broadcasted_iota(jnp.int32, (tile, tile), 1)

    def chosen(flags):
        return jnp.where(flags, 1.0, 0.0).astype(BF16)

    col_lines, row_lines = (padded[0].astype(BF16), padded[1].astype(BF16))
    last = taps - 1
    lines[0] = dot(row_lines, chosen((tap_ids + places == tile) | (tap_ids + places == 0)))
    lines[1] = dot(
        row_lines, chosen((places - tap_ids == tile - last) | (tap_ids - places == last))
    )
    lines[2] = dot(col_lines, chosen(tap_ids + places == last))
    masks[0] = chosen(tap_ids >= places)
    masks[1] = chosen(tap_ids < places)
    masks[2] = chosen(tap_ids <= places)
    masks[3] = chosen(tap_ids > jnp.where(places < two, places, places - two))

    def rolled(line, count):
        return pltpu.roll(
            jnp.broadcast_to(line, (count, tile)), 0, 1, stride=1, stride_axis=0
        )

    def circulant(table, k, part):
        return rolled(lines[table, pl.ds(parts * k + part, 1), :], tile)

    def build_cols(k, carry):
        for part in range(parts):
            line = padded[0, pl.ds(parts * k + part, 1), :]
            col_mats[k, part * two : (part + 1) * two, :] = rolled(line, two).astype(BF16)
        return carry

    def triangles(table, k, kept):
        t0, t1 = (circulant(table, k, part).astype(BF16) for part in range(parts))
        for side in range(2):
            a1 = t1 * masks[side]
            kept[k, side, 0] = t0 * masks[side]
            kept[k, side, 1] = a1
            kept[k, side, 2] = -a1

    def build_rows(k, carry):
        triangles(0, k, row_mats)
        return carry

    def build_adjoints(k):
        triangles(1, k, row_adjoints)
        u0, u1 = (circulant(2, k, part) for part in range(parts))
        col_adjoints[k, :, :tile] = u0.astype(BF16) * masks[2]
        col_adjoints[k, :, tile : 2 * tile] = u1.astype(BF16) * masks[2]
        mixed = jnp.where(places < two, u0, pltpu.roll(u1, two, 1)).astype(BF16)
        col_adjoints[k, :, 2 * tile :] = mixed * masks[3]

    def square(kept, k, side, top, bottom):
        plain = kept[k, side, 0]
        return jnp.concatenate(
            [
                jnp.concatenate([plain, kept[k, side, top]], axis=1),
                jnp.concatenate([kept[k, side, bottom], plain], axis=1),
            ],
            axis=0,
        )

    lax.fori_loop(0, kernels, build_cols, 0)

    pl.semaphore_wait(barrier, group - 1)

    for number, (down, right) in enumerate(DIRECTIONS):

        @pl.when(inside(down, right))
        def _():
            transfer(number).start()

    lax.fori_loop(0, kernels, build_rows, 0)
    intensity[...] = jnp.zeros_like(intensity)
    descent[...] = jnp.zeros_like(descent)

    for number, (down, right) in enumerate(DIRECTIONS):

        @pl.when(inside(down, right))
        def _():
            transfer(number).wait_send()

        @pl.when(inside(-down, -right))
        def _():
            transfer(number).wait_recv()

    lanes = halo.shape[2]
    reach = rows + tile
    shifted = pltpu.roll(halo[0].astype(F32), lanes - two, 1)[:, :reach].astype(BF16)
    steps = wide // two
    for step in range(steps):
        windows[:, step * reach : (step + 1) * reach] = shifted[step * two : step * two + tile]

    batch = next(size for size in (4, 3, 2, 1) if kernels % size == 0)

    def col_pass(j, held):
        first = j * batch
        made = dot(
            col_mats[pl.ds(first, batch)].reshape(batch * parts * two, tile), windows[...]
        ).astype(BF16)
        for i in range(batch):
            for part in range(parts):
                top = (i * parts + part) * two
                for step in range(steps):
                    for band in range(bands + 1):
                        lane = step * reach + band * tile
                        held[
                            i,
                            band,
                            step * two : (step + 1) * two,
                            part * tile : (part + 1) * tile,
                        ] = made[top : top + two, lane : lane + tile]

    def row_pass(k, columns):
        weight = weight_ref[k]
        held = [columns[band] for band in range(bands + 1)]
        joined = jnp.concatenate(
            [jnp.concatenate(held[band : band + 2], axis=1) for band in range(bands)], axis=0
        )
        first, second = (square(row_mats, k, side, 1, 2) for side in range(2))
        whole = dot(joined, jnp.concatenate([first, second], axis=0))
        tail = dot(held[bands], first)
        for band in range(bands + 1):
            pair = tail if band == bands else whole[band * wide : (band + 1) * wide]
            fields[k, band] = pair.astype(BF16)
            real_part, imag_part = (pair[:, :tile], pair[:, tile:])
            intensity[band] += weight * (real_part * real_part + imag_part * imag_part)

    def row_passes(j, held):
        for i in range(batch):
            row_pass(j * batch + i, held.at[i])
            build_adjoints(j * batch + i)

    def in_pairs(make, take, count, helds):
        make(0, helds[0])
        size = next(size for size in (4, 2, 1) if count % size == 0)

        def step(j, carry):
            for i in range(size):
                k = size * j + i
                if size == 1:
                    take(k, helds[0])
                make(jnp.minimum(k + 1, count - 1), helds[(i + 1) % 2 if size > 1 else 0])
                if size > 1:
                    take(k, helds[i % 2])
            return carry

        lax.fori_loop(0, count // size, step, 0)

    in_pairs(col_pass, row_passes, kernels // batch, (even_columns, odd_columns))

    swap = pltpu.make_async_remote_copy(
        src_ref=intensity,
        dst_ref=other,
        send_sem=expo_send,
        recv_sem=expo_recv,
        device_id={"expo": 1 - expo},
        device_id_type=MESH,
    )
    swap.start()
    swap.wait()

    def side_by_side(ref):
        return jnp.concatenate([ref[band] for band in range(bands + 1)], axis=1)

    total = side_by_side(intensity) + side_by_side(other)
    resist = jax.nn.sigmoid(resist_steep * (total - resist_level))
    target_ext = pltpu.roll(
        halo[1, half : half + wide, :].astype(F32), lanes - (tile - half), 1
    )[:, :reach]
    row_lanes = lax.broadcasted_iota(jnp.int32, (wide, reach), 1)
    row_ids = row_lanes + (strip * rows - half)
    col_ids = lax.broadcasted_iota(jnp.int32, (wide, reach), 0) + (col * width - half)
    kept = (
        (row_ids >= 0)
        & (row_ids < strips * rows)
        & (col_ids >= 0)
        & (col_ids < cols * width)
        & (row_lanes < rows + two)
    )
    mismatch = resist - target_ext
    steepness = jnp.where(kept, 2.0 * mismatch * resist_steep * resist * (1.0 - resist), 0.0)
    for band in range(bands + 1):
        slope[band] = steepness[:, band * tile : (band + 1) * tile]
    own = pltpu.roll(resist[half : half + width, :], reach - half, 1)[:, :rows].T
    resist_ref[...] = own
    own_miss = own - target_ref[...].astype(F32)
    loss_line = jnp.sum(own_miss * own_miss, axis=0, keepdims=True)

    def correlate(k, held):
        scale = 2.0 * weight_ref[k]
        products = []
        for band in range(bands + 1):
            weighting = (scale * slope[band]).astype(BF16)
            products.append(fields[k, band] * jnp.concatenate([weighting] * parts, axis=1))
        joined = jnp.concatenate(
            [jnp.concatenate(products[band : band + 2], axis=1) for band in range(bands)], axis=0
        )
        matrix = jnp.concatenate(
            [square(row_adjoints, k, side, 2, 1) for side in range(2)], axis=0
        )
        returned = dot(joined, matrix).astype(BF16)
        for band in range(bands):
            held[band] = returned[band * wide : (band + 1) * wide]

    def gather(k, held):
        found = [
            jnp.concatenate(
                [held[band, :, part * tile : (part + 1) * tile] for band in range(bands)], axis=1
            )
            for part in range(parts)
        ]
        source = jnp.concatenate([f[:tile] for f in found] + [f[tile:] for f in found], axis=0)
        descent[...] += dot(col_adjoints[k], source)

    in_pairs(correlate, gather, kernels, (even, odd))

    mask = jax.nn.sigmoid(mask_slope * params_ref[0])
    gradient = descent[...].T * mask_slope * mask * (1.0 - mask)
    steps_ref[...] = gradient
    square_line = jnp.sum(gradient * gradient, axis=0, keepdims=True)
    which = lax.broadcasted_iota(jnp.int32, partial.shape, 0)
    sums = jnp.where(which == 0, loss_line, jnp.where(which == 1, square_line, 0.0))
    partial[...] = sums
    slots[me] = sums

    shares, arrivals = ([], [])
    for number, (place, index) in enumerate(peers):
        for found, slot in ((shares, me), (arrivals, index)):
            found.append(
                pltpu.make_async_remote_copy(
                    src_ref=partial,
                    dst_ref=slots.at[slot],
                    send_sem=sum_send.at[number],
                    recv_sem=sum_recv.at[slot],
                    device_id=place,
                    device_id_type=MESH,
                )
            )
    for share in shares:
        share.start()
    for arrival in arrivals:
        arrival.wait()

    totals_ref[...] = jnp.sum(slots[...], axis=0)


def finish(copies, params_ref, steps_ref, resist_in, totals_ref, new_ref, resist_ref, loss_ref):
    expos, blocks = copies
    rows, width = resist_in.shape
    pixels = rows * width * blocks
    loss_ref[0] = jnp.sum(totals_ref[0:1, :]) / (expos * pixels)
    square_sum = jnp.sum(totals_ref[1:2, :], axis=1, keepdims=True)
    root_mean = jnp.sqrt(square_sum / (expos * pixels) + norm_eps)
    new_ref[0] = params_ref[0] - step_length * steps_ref[...] / root_mean
    resist_ref[...] = resist_in[...]


def shards(mask_params, target, col_taps, row_taps, kernel_weights):
    rows, width = target.shape
    kernels, _, taps = col_taps.shape
    half = taps // 2
    two = 2 * half
    tile, wide, bands = (2 * two, width + two, rows // (2 * two))
    strips, cols, expos = (lax.axis_size(a) for a in ("strip", "col", "expo"))
    group = strips * cols * expos
    vmem = pl.BlockSpec(memory_space=pltpu.VMEM)
    smem = pl.BlockSpec(memory_space=pltpu.SMEM)
    dma = pltpu.SemaphoreType.DMA
    image = jax.ShapeDtypeStruct(target.shape, F32)
    batch = next(size for size in (4, 3, 2, 1) if kernels % size == 0)
    anywhere = pl.BlockSpec(memory_space=pl.ANY)
    steps, resist, totals = pl.pallas_call(
        functools.partial(body, (strips, cols, expos, half)),
        out_shape=(image, image, jax.ShapeDtypeStruct((8, width), F32)),
        in_specs=[anywhere, anywhere, vmem, vmem, smem],
        out_specs=(vmem, vmem, vmem),
        scratch_shapes=[
            pltpu.VMEM(mask_params.shape, F32),
            pltpu.VMEM(target.shape, target.dtype),
            pltpu.VMEM((2, width + 2 * two, rows + 2 * tile), BF16),
            pltpu.VMEM((tile, (wide // two) * (rows + tile)), BF16),
            pltpu.VMEM((2, 2 * kernels, tile), F32),
            pltpu.VMEM((3, 2 * kernels, tile), F32),
            pltpu.VMEM((4, tile, tile), BF16),
            pltpu.VMEM((kernels, 2 * two, tile), BF16),
            pltpu.VMEM((kernels, 2, 3, tile, tile), BF16),
            pltpu.VMEM((kernels, 2, 3, tile, tile), BF16),
            pltpu.VMEM((kernels, width, 3 * tile), BF16),
            pltpu.VMEM((batch, bands + 1, wide, 2 * tile), BF16),
            pltpu.VMEM((batch, bands + 1, wide, 2 * tile), BF16),
            pltpu.VMEM((kernels, bands + 1, wide, 2 * tile), BF16),
            pltpu.VMEM((bands + 1, wide, tile), F32),
            pltpu.VMEM((bands + 1, wide, tile), F32),
            pltpu.VMEM((bands + 1, wide, tile), F32),
            pltpu.VMEM((bands, wide, 2 * tile), BF16),
            pltpu.VMEM((bands, wide, 2 * tile), BF16),
            pltpu.VMEM((width, rows), F32),
            pltpu.VMEM((8, width), F32),
            pltpu.VMEM((group, 8, width), F32),
            dma((2,)),
            dma((8,)),
            dma((8,)),
            dma,
            dma,
            dma((group,)),
            dma((group,)),
        ],
        compiler_params=pltpu.CompilerParams(
            collective_id=0, has_side_effects=True, vmem_limit_bytes=56 * 1024 * 1024
        ),
    )(mask_params, target, col_taps, row_taps, kernel_weights)
    return pl.pallas_call(
        functools.partial(finish, (expos, strips * cols)),
        out_shape=(
            jax.ShapeDtypeStruct(mask_params.shape, F32),
            image,
            jax.ShapeDtypeStruct((1,), F32),
        ),
        in_specs=[vmem] * 4,
        out_specs=(vmem, vmem, smem),
    )(mask_params, steps, resist, totals)


def solution(mesh):
    return jax.shard_map(
        shards,
        mesh=mesh,
        in_specs=(
            P("expo", ("tiles", "strip"), "col"),
            P(("tiles", "strip"), "col"),
            P(),
            P(),
            P(),
        ),
        out_specs=(P("expo", ("tiles", "strip"), "col"), P(("tiles", "strip"), "col"), P("tiles")),
        check_vma=False,
    )
```

```python
import functools

import jax
import jax.numpy as jnp
from jax import lax
from jax.experimental import pallas as pl
from jax.experimental.pallas import tpu as pltpu
from jax.sharding import PartitionSpec as P

mask_slope = 4.0
resist_steep = 4.0
resist_level = 3.0
step_length = 0.5
norm_eps = 1e-06

MESH = pl.DeviceIdType.MESH
F32 = jnp.float32
BF16 = jnp.bfloat16
DIRECTIONS = [(a, b) for a in (-1, 0, 1) for b in (-1, 0, 1) if (a, b) != (0, 0)]


def dot(a, b):
    return jnp.dot(a, b, preferred_element_type=F32)


def body(
    sizes,
    params_hbm,
    target_hbm,
    col_ref,
    row_ref,
    weight_ref,
    steps_ref,
    resist_ref,
    totals_ref,
    params_ref,
    target_ref,
    halo,
    windows,
    padded,
    lines,
    masks,
    col_mats,
    row_mats,
    row_adjoints,
    col_adjoints,
    even_columns,
    odd_columns,
    fields,
    intensity,
    other,
    slope,
    even,
    odd,
    descent,
    partial,
    slots,
    fetch_sem,
    halo_send,
    halo_recv,
    expo_send,
    expo_recv,
    sum_send,
    sum_recv,
):
    strips, cols, expos, half = sizes
    kernels, parts, taps = col_ref.shape
    rows, width = target_ref.shape
    two = 2 * half
    tile = 2 * two
    wide = width + two
    bands = rows // tile
    group = strips * cols * expos
    strip, col, expo = (lax.axis_index("strip"), lax.axis_index("col"), lax.axis_index("expo"))
    me = (strip * cols + col) * expos + expo

    def beyond(index, step, count):
        moved = index + step
        return jnp.where(moved >= count, moved - count, moved)

    peers = []
    for number in range(1, group):
        steps_to = (number // (cols * expos), number // expos % cols, number % expos)
        there = [
            beyond(index, step, count) if step else index
            for index, step, count in zip((strip, col, expo), steps_to, sizes[:3])
        ]
        peers.append(
            (
                dict(zip(("strip", "col", "expo"), there)),
                (there[0] * cols + there[1]) * expos + there[2],
            )
        )

    fetches = [
        pltpu.make_async_copy(source, into, fetch_sem.at[number])
        for number, (source, into) in enumerate(
            ((params_hbm, params_ref), (target_hbm, target_ref))
        )
    ]
    for fetch in fetches:
        fetch.start()

    halo[...] = jnp.zeros_like(halo)

    barrier = pltpu.get_barrier_semaphore()

    for place, _ in peers:
        pl.semaphore_signal(barrier, inc=1, device_id=place, device_id_type=MESH)

    for fetch in fetches:
        fetch.wait()
    mask = jax.nn.sigmoid(mask_slope * params_ref[0])
    halo[0, two : two + width, tile : tile + rows] = mask.T.astype(BF16)
    target_now = target_ref[...].astype(F32)
    halo[1, two : two + width, tile : tile + rows] = target_now.T.astype(BF16)

    def transfer(plane, number):
        down, right = DIRECTIONS[number]
        lane, lanes, to_lane = {
            -1: (tile, tile, tile + rows),
            0: (tile, rows, tile),
            1: (rows, tile, 0),
        }[down]
        place, places, to_place = {
            -1: (two, two, two + width),
            0: (two, width, two),
            1: (width, two, 0),
        }[right]
        return pltpu.make_async_remote_copy(
            src_ref=halo.at[plane, pl.ds(place, places), pl.ds(lane, lanes)],
            dst_ref=halo.at[plane, pl.ds(to_place, places), pl.ds(to_lane, lanes)],
            send_sem=halo_send.at[plane, number],
            recv_sem=halo_recv.at[plane, number],
            device_id={
                "strip": jnp.clip(strip + down, 0, strips - 1),
                "col": jnp.clip(col + right, 0, cols - 1),
            },
            device_id_type=MESH,
        )

    def inside(down, right):
        to_strip, to_col = (strip + down, col + right)
        return (to_strip >= 0) & (to_strip < strips) & (to_col >= 0) & (to_col < cols)

    padded[...] = jnp.zeros_like(padded)
    for k in range(kernels):
        for table, source in enumerate((col_ref, row_ref)):
            padded[table, parts * k : parts * (k + 1), :taps] = source[k].astype(F32)
    tap_ids = lax.broadcasted_iota(jnp.int32, (tile, tile), 0)
    places = lax.broadcasted_iota(jnp.int32, (tile, tile), 1)

    def chosen(flags):
        return jnp.where(flags, 1.0, 0.0).astype(BF16)

    col_lines, row_lines = (padded[0].astype(BF16), padded[1].astype(BF16))
    last = taps - 1
    lines[0] = dot(row_lines, chosen((tap_ids + places == tile) | (tap_ids + places == 0)))
    lines[1] = dot(
        row_lines, chosen((places - tap_ids == tile - last) | (tap_ids - places == last))
    )
    lines[2] = dot(col_lines, chosen(tap_ids + places == last))
    masks[0] = chosen(tap_ids >= places)
    masks[1] = chosen(tap_ids < places)
    masks[2] = chosen(tap_ids <= places)
    masks[3] = chosen(tap_ids > jnp.where(places < two, places, places - two))

    def rolled(line, count):
        return pltpu.roll(
            jnp.broadcast_to(line, (count, tile)), 0, 1, stride=1, stride_axis=0
        )

    def circulant(table, k, part):
        return rolled(lines[table, pl.ds(parts * k + part, 1), :], tile)

    def build_cols(k, carry):
        for part in range(parts):
            line = padded[0, pl.ds(parts * k + part, 1), :]
            col_mats[k, part * two : (part + 1) * two, :] = rolled(line, two).astype(BF16)
        return carry

    def triangles(table, k, kept):
        t0, t1 = (circulant(table, k, part).astype(BF16) for part in range(parts))
        for side in range(2):
            a1 = t1 * masks[side]
            kept[k, side, 0] = t0 * masks[side]
            kept[k, side, 1] = a1
            kept[k, side, 2] = -a1

    def build_rows(k, carry):
        triangles(0, k, row_mats)
        return carry

    def build_adjoints(k):
        triangles(1, k, row_adjoints)
        u0, u1 = (circulant(2, k, part) for part in range(parts))
        col_adjoints[k, :, :tile] = u0.astype(BF16) * masks[2]
        col_adjoints[k, :, tile : 2 * tile] = u1.astype(BF16) * masks[2]
        mixed = jnp.where(places < two, u0, pltpu.roll(u1, two, 1)).astype(BF16)
        col_adjoints[k, :, 2 * tile :] = mixed * masks[3]

    def square(kept, k, side, top, bottom):
        plain = kept[k, side, 0]
        return jnp.concatenate(
            [
                jnp.concatenate([plain, kept[k, side, top]], axis=1),
                jnp.concatenate([kept[k, side, bottom], plain], axis=1),
            ],
            axis=0,
        )

    lax.fori_loop(0, kernels, build_cols, 0)

    pl.semaphore_wait(barrier, group - 1)

    for plane in range(2):
        for number, (down, right) in enumerate(DIRECTIONS):

            @pl.when(inside(down, right))
            def _():
                transfer(plane, number).start()

    lax.fori_loop(0, kernels, build_rows, 0)
    intensity[...] = jnp.zeros_like(intensity)
    descent[...] = jnp.zeros_like(descent)

    def receive(plane):
        for number, (down, right) in enumerate(DIRECTIONS):

            @pl.when(inside(down, right))
            def _():
                transfer(plane, number).wait_send()

            @pl.when(inside(-down, -right))
            def _():
                transfer(plane, number).wait_recv()

    receive(0)

    lanes = halo.shape[2]
    reach = rows + tile
    shifted = pltpu.roll(halo[0].astype(F32), lanes - two, 1)[:, :reach].astype(BF16)
    steps = wide // two
    for step in range(steps):
        windows[:, step * reach : (step + 1) * reach] = shifted[step * two : step * two + tile]

    batch = next(size for size in (4, 3, 2, 1) if kernels % size == 0)

    def col_pass(j, held):
        first = j * batch
        made = dot(
            col_mats[pl.ds(first, batch)].reshape(batch * parts * two, tile), windows[...]
        ).astype(BF16)
        for i in range(batch):
            for part in range(parts):
                top = (i * parts + part) * two
                for step in range(steps):
                    for band in range(bands + 1):
                        lane = step * reach + band * tile
                        held[
                            i,
                            band,
                            step * two : (step + 1) * two,
                            part * tile : (part + 1) * tile,
                        ] = made[top : top + two, lane : lane + tile]

    def row_pass(k, columns):
        weight = weight_ref[k]
        held = [columns[band] for band in range(bands + 1)]
        joined = jnp.concatenate(
            [jnp.concatenate(held[band : band + 2], axis=1) for band in range(bands)], axis=0
        )
        first, second = (square(row_mats, k, side, 1, 2) for side in range(2))
        whole = dot(joined, jnp.concatenate([first, second], axis=0))
        tail = dot(held[bands], first)
        for band in range(bands + 1):
            pair = tail if band == bands else whole[band * wide : (band + 1) * wide]
            fields[k, band] = pair.astype(BF16)
            real_part, imag_part = (pair[:, :tile], pair[:, tile:])
            intensity[band] += weight * (real_part * real_part + imag_part * imag_part)

    def row_passes(j, held):
        for i in range(batch):
            row_pass(j * batch + i, held.at[i])
            if i % 2 == 0:
                build_adjoints(j * batch + i)

    def in_pairs(make, take, count, helds):
        make(0, helds[0])
        size = next(size for size in (4, 2, 1) if count % size == 0)

        def step(j, carry):
            for i in range(size):
                k = size * j + i
                if size == 1:
                    take(k, helds[0])
                make(jnp.minimum(k + 1, count - 1), helds[(i + 1) % 2 if size > 1 else 0])
                if size > 1:
                    take(k, helds[i % 2])
            return carry

        lax.fori_loop(0, count // size, step, 0)

    in_pairs(col_pass, row_passes, kernels // batch, (even_columns, odd_columns))

    swap = pltpu.make_async_remote_copy(
        src_ref=intensity,
        dst_ref=other,
        send_sem=expo_send,
        recv_sem=expo_recv,
        device_id={"expo": 1 - expo},
        device_id_type=MESH,
    )
    swap.start()

    def build_others(j, carry):
        for i in range(1, batch, 2):
            build_adjoints(j * batch + i)
        return carry

    lax.fori_loop(0, kernels // batch, build_others, 0)
    receive(1)
    swap.wait()

    def side_by_side(ref):
        return jnp.concatenate([ref[band] for band in range(bands + 1)], axis=1)

    total = side_by_side(intensity) + side_by_side(other)
    resist = jax.nn.sigmoid(resist_steep * (total - resist_level))
    target_ext = pltpu.roll(
        halo[1, half : half + wide, :].astype(F32), lanes - (tile - half), 1
    )[:, :reach]
    row_lanes = lax.broadcasted_iota(jnp.int32, (wide, reach), 1)
    row_ids = row_lanes + (strip * rows - half)
    col_ids = lax.broadcasted_iota(jnp.int32, (wide, reach), 0) + (col * width - half)
    kept = (
        (row_ids >= 0)
        & (row_ids < strips * rows)
        & (col_ids >= 0)
        & (col_ids < cols * width)
        & (row_lanes < rows + two)
    )
    mismatch = resist - target_ext
    steepness = jnp.where(kept, 2.0 * mismatch * resist_steep * resist * (1.0 - resist), 0.0)
    for band in range(bands + 1):
        slope[band] = steepness[:, band * tile : (band + 1) * tile]
    own = pltpu.roll(resist[half : half + width, :], reach - half, 1)[:, :rows].T
    resist_ref[...] = own
    own_miss = own - target_ref[...].astype(F32)
    loss_line = jnp.sum(own_miss * own_miss, axis=0, keepdims=True)

    def correlate(k, held):
        scale = 2.0 * weight_ref[k]
        products = []
        for band in range(bands + 1):
            weighting = (scale * slope[band]).astype(BF16)
            products.append(fields[k, band] * jnp.concatenate([weighting] * parts, axis=1))
        joined = jnp.concatenate(
            [jnp.concatenate(products[band : band + 2], axis=1) for band in range(bands)], axis=0
        )
        matrix = jnp.concatenate(
            [square(row_adjoints, k, side, 2, 1) for side in range(2)], axis=0
        )
        returned = dot(joined, matrix).astype(BF16)
        for band in range(bands):
            held[band] = returned[band * wide : (band + 1) * wide]

    def correlate_all(j, held):
        for i in range(batch):
            correlate(j * batch + i, held.at[i])

    def gather_all(j, held):
        sources = []
        for i in range(batch):
            found = [
                jnp.concatenate(
                    [
                        held[i, band, :, part * tile : (part + 1) * tile]
                        for band in range(bands)
                    ],
                    axis=1,
                )
                for part in range(parts)
            ]
            sources += [f[:tile] for f in found] + [f[tile:] for f in found]
        matrix = jnp.concatenate([col_adjoints[j * batch + i] for i in range(batch)], axis=1)
        descent[...] += dot(matrix, jnp.concatenate(sources, axis=0))

    in_pairs(correlate_all, gather_all, kernels // batch, (even, odd))

    mask = jax.nn.sigmoid(mask_slope * params_ref[0])
    gradient = descent[...].T * mask_slope * mask * (1.0 - mask)
    steps_ref[...] = gradient
    square_line = jnp.sum(gradient * gradient, axis=0, keepdims=True)
    which = lax.broadcasted_iota(jnp.int32, partial.shape, 0)
    sums = jnp.where(which == 0, loss_line, jnp.where(which == 1, square_line, 0.0))
    partial[...] = sums
    slots[me] = sums

    shares, arrivals = ([], [])
    for number, (place, index) in enumerate(peers):
        for found, slot in ((shares, me), (arrivals, index)):
            found.append(
                pltpu.make_async_remote_copy(
                    src_ref=partial,
                    dst_ref=slots.at[slot],
                    send_sem=sum_send.at[number],
                    recv_sem=sum_recv.at[slot],
                    device_id=place,
                    device_id_type=MESH,
                )
            )
    for share in shares:
        share.start()
    for arrival in arrivals:
        arrival.wait()

    totals_ref[...] = jnp.sum(slots[...], axis=0)


def finish(
    copies, params_ref, steps_ref, resist_in, totals_ref, new_ref, resist_ref, loss_ref, sem
):
    passing = pltpu.make_async_copy(resist_in, resist_ref, sem)
    passing.start()
    expos, blocks = copies
    rows, width = steps_ref.shape
    pixels = rows * width * blocks
    loss_ref[0] = jnp.sum(totals_ref[0:1, :]) / (expos * pixels)
    square_sum = jnp.sum(totals_ref[1:2, :], axis=1, keepdims=True)
    root_mean = jnp.sqrt(square_sum / (expos * pixels) + norm_eps)
    new_ref[0] = params_ref[0] - step_length * steps_ref[...] / root_mean
    passing.wait()


def shards(mask_params, target, col_taps, row_taps, kernel_weights):
    rows, width = target.shape
    kernels, _, taps = col_taps.shape
    half = taps // 2
    two = 2 * half
    tile, wide, bands = (2 * two, width + two, rows // (2 * two))
    strips, cols, expos = (lax.axis_size(a) for a in ("strip", "col", "expo"))
    group = strips * cols * expos
    vmem = pl.BlockSpec(memory_space=pltpu.VMEM)
    smem = pl.BlockSpec(memory_space=pltpu.SMEM)
    dma = pltpu.SemaphoreType.DMA
    image = jax.ShapeDtypeStruct(target.shape, F32)
    batch = next(size for size in (4, 3, 2, 1) if kernels % size == 0)
    anywhere = pl.BlockSpec(memory_space=pl.ANY)
    steps, resist, totals = pl.pallas_call(
        functools.partial(body, (strips, cols, expos, half)),
        out_shape=(image, image, jax.ShapeDtypeStruct((8, width), F32)),
        in_specs=[anywhere, anywhere, vmem, vmem, smem],
        out_specs=(vmem, vmem, vmem),
        scratch_shapes=[
            pltpu.VMEM(mask_params.shape, F32),
            pltpu.VMEM(target.shape, target.dtype),
            pltpu.VMEM((2, width + 2 * two, rows + 2 * tile), BF16),
            pltpu.VMEM((tile, (wide // two) * (rows + tile)), BF16),
            pltpu.VMEM((2, 2 * kernels, tile), F32),
            pltpu.VMEM((3, 2 * kernels, tile), F32),
            pltpu.VMEM((4, tile, tile), BF16),
            pltpu.VMEM((kernels, 2 * two, tile), BF16),
            pltpu.VMEM((kernels, 2, 3, tile, tile), BF16),
            pltpu.VMEM((kernels, 2, 3, tile, tile), BF16),
            pltpu.VMEM((kernels, width, 3 * tile), BF16),
            pltpu.VMEM((batch, bands + 1, wide, 2 * tile), BF16),
            pltpu.VMEM((batch, bands + 1, wide, 2 * tile), BF16),
            pltpu.VMEM((kernels, bands + 1, wide, 2 * tile), BF16),
            pltpu.VMEM((bands + 1, wide, tile), F32),
            pltpu.VMEM((bands + 1, wide, tile), F32),
            pltpu.VMEM((bands + 1, wide, tile), F32),
            pltpu.VMEM((batch, bands, wide, 2 * tile), BF16),
            pltpu.VMEM((batch, bands, wide, 2 * tile), BF16),
            pltpu.VMEM((width, rows), F32),
            pltpu.VMEM((8, width), F32),
            pltpu.VMEM((group, 8, width), F32),
            dma((2,)),
            dma((2, 8)),
            dma((2, 8)),
            dma,
            dma,
            dma((group,)),
            dma((group,)),
        ],
        compiler_params=pltpu.CompilerParams(
            collective_id=0, has_side_effects=True, vmem_limit_bytes=56 * 1024 * 1024
        ),
    )(mask_params, target, col_taps, row_taps, kernel_weights)
    return pl.pallas_call(
        functools.partial(finish, (expos, strips * cols)),
        out_shape=(
            jax.ShapeDtypeStruct(mask_params.shape, F32),
            image,
            jax.ShapeDtypeStruct((1,), F32),
        ),
        in_specs=[vmem, vmem, anywhere, vmem],
        out_specs=(vmem, anywhere, smem),
        scratch_shapes=[dma],
    )(mask_params, steps, resist, totals)


def solution(mesh):
    return jax.shard_map(
        shards,
        mesh=mesh,
        in_specs=(
            P("expo", ("tiles", "strip"), "col"),
            P(("tiles", "strip"), "col"),
            P(),
            P(),
            P(),
        ),
        out_specs=(P("expo", ("tiles", "strip"), "col"), P(("tiles", "strip"), "col"), P("tiles")),
        check_vma=False,
    )
```

```python
import functools

import jax
import jax.numpy as jnp
from jax import lax
from jax.experimental import pallas as pl
from jax.experimental.pallas import tpu as pltpu
from jax.sharding import PartitionSpec as P

mask_slope = 4.0
resist_steep = 4.0
resist_level = 3.0
step_length = 0.5
norm_eps = 1e-06

MESH = pl.DeviceIdType.MESH
F32 = jnp.float32
BF16 = jnp.bfloat16
DIRECTIONS = [(a, b) for a in (-1, 0, 1) for b in (-1, 0, 1) if (a, b) != (0, 0)]


def dot(a, b):
    return jnp.dot(a, b, preferred_element_type=F32)


def body(
    sizes,
    params_hbm,
    target_hbm,
    col_hbm,
    row_hbm,
    weight_hbm,
    steps_ref,
    resist_ref,
    totals_ref,
    params_ref,
    target_ref,
    col_ref,
    row_ref,
    weight_ref,
    halo,
    windows,
    padded,
    lines,
    masks,
    col_mats,
    row_mats,
    row_adjoints,
    col_adjoints,
    even_columns,
    odd_columns,
    fields,
    intensity,
    other,
    slope,
    even,
    odd,
    descent,
    shown,
    partial,
    slots,
    fetch_sem,
    halo_send,
    halo_recv,
    expo_send,
    expo_recv,
    sum_send,
    sum_recv,
):
    strips, cols, expos, half = sizes
    kernels, parts, taps = col_ref.shape
    rows, width = target_ref.shape
    two = 2 * half
    tile = 2 * two
    wide = width + two
    bands = rows // tile
    group = strips * cols * expos
    strip, col, expo = (lax.axis_index("strip"), lax.axis_index("col"), lax.axis_index("expo"))
    me = (strip * cols + col) * expos + expo

    def beyond(index, step, count):
        moved = index + step
        return jnp.where(moved >= count, moved - count, moved)

    peers = []
    for number in range(1, group):
        steps_to = (number // (cols * expos), number // expos % cols, number % expos)
        there = [
            beyond(index, step, count) if step else index
            for index, step, count in zip((strip, col, expo), steps_to, sizes[:3])
        ]
        peers.append(
            (
                dict(zip(("strip", "col", "expo"), there)),
                (there[0] * cols + there[1]) * expos + there[2],
            )
        )

    fetches = [
        pltpu.make_async_copy(source, into, fetch_sem.at[number])
        for number, (source, into) in enumerate(
            (
                (params_hbm, params_ref),
                (target_hbm, target_ref),
                (col_hbm, col_ref),
                (row_hbm, row_ref),
                (weight_hbm, weight_ref),
            )
        )
    ]
    for fetch in fetches:
        fetch.start()

    halo[...] = jnp.zeros_like(halo)

    barrier = pltpu.get_barrier_semaphore()

    for place, _ in peers:
        pl.semaphore_signal(barrier, inc=1, device_id=place, device_id_type=MESH)

    for fetch in fetches[:2]:
        fetch.wait()
    mask = jax.nn.sigmoid(mask_slope * params_ref[0])
    halo[0, two : two + width, tile : tile + rows] = mask.T.astype(BF16)
    target_now = target_ref[...].astype(F32)
    halo[1, two : two + width, tile : tile + rows] = target_now.T.astype(BF16)

    def transfer(plane, number):
        down, right = DIRECTIONS[number]
        lane, lanes, to_lane = {
            -1: (tile, tile, tile + rows),
            0: (tile, rows, tile),
            1: (rows, tile, 0),
        }[down]
        place, places, to_place = {
            -1: (two, two, two + width),
            0: (two, width, two),
            1: (width, two, 0),
        }[right]
        return pltpu.make_async_remote_copy(
            src_ref=halo.at[plane, pl.ds(place, places), pl.ds(lane, lanes)],
            dst_ref=halo.at[plane, pl.ds(to_place, places), pl.ds(to_lane, lanes)],
            send_sem=halo_send.at[plane, number],
            recv_sem=halo_recv.at[plane, number],
            device_id={
                "strip": jnp.clip(strip + down, 0, strips - 1),
                "col": jnp.clip(col + right, 0, cols - 1),
            },
            device_id_type=MESH,
        )

    def inside(down, right):
        to_strip, to_col = (strip + down, col + right)
        return (to_strip >= 0) & (to_strip < strips) & (to_col >= 0) & (to_col < cols)

    pl.semaphore_wait(barrier, group - 1)

    for plane in range(2):
        for number, (down, right) in enumerate(DIRECTIONS):

            @pl.when(inside(down, right))
            def _():
                transfer(plane, number).start()

    for fetch in fetches[2:]:
        fetch.wait()
    padded[...] = jnp.zeros_like(padded)
    for k in range(kernels):
        for table, source in enumerate((col_ref, row_ref)):
            padded[table, parts * k : parts * (k + 1), :taps] = source[k].astype(F32)
    tap_ids = lax.broadcasted_iota(jnp.int32, (tile, tile), 0)
    places = lax.broadcasted_iota(jnp.int32, (tile, tile), 1)

    def chosen(flags):
        return jnp.where(flags, 1.0, 0.0).astype(BF16)

    col_lines, row_lines = (padded[0].astype(BF16), padded[1].astype(BF16))
    last = taps - 1
    lines[0] = dot(row_lines, chosen((tap_ids + places == tile) | (tap_ids + places == 0)))
    lines[1] = dot(
        row_lines, chosen((places - tap_ids == tile - last) | (tap_ids - places == last))
    )
    lines[2] = dot(col_lines, chosen(tap_ids + places == last))
    masks[0] = chosen(tap_ids >= places)
    masks[1] = chosen(tap_ids < places)
    masks[2] = chosen(tap_ids <= places)
    masks[3] = chosen(tap_ids > jnp.where(places < two, places, places - two))

    def rolled(line, count):
        return pltpu.roll(
            jnp.broadcast_to(line, (count, tile)), 0, 1, stride=1, stride_axis=0
        )

    def circulant(table, k, part):
        return rolled(lines[table, pl.ds(parts * k + part, 1), :], tile)

    def build_cols(k, carry):
        for part in range(parts):
            line = padded[0, pl.ds(parts * k + part, 1), :]
            col_mats[k, part * two : (part + 1) * two, :] = rolled(line, two).astype(BF16)
        return carry

    def triangles(table, k, kept):
        t0, t1 = (circulant(table, k, part).astype(BF16) for part in range(parts))
        for side in range(2):
            a1 = t1 * masks[side]
            kept[k, side, 0] = t0 * masks[side]
            kept[k, side, 1] = a1
            kept[k, side, 2] = -a1

    def build_rows(k, carry):
        triangles(0, k, row_mats)
        return carry

    def build_adjoints(k):
        triangles(1, k, row_adjoints)
        u0, u1 = (circulant(2, k, part) for part in range(parts))
        col_adjoints[k, :, :tile] = u0.astype(BF16) * masks[2]
        col_adjoints[k, :, tile : 2 * tile] = u1.astype(BF16) * masks[2]
        mixed = jnp.where(places < two, u0, pltpu.roll(u1, two, 1)).astype(BF16)
        col_adjoints[k, :, 2 * tile :] = mixed * masks[3]

    def square(kept, k, side, top, bottom):
        plain = kept[k, side, 0]
        return jnp.concatenate(
            [
                jnp.concatenate([plain, kept[k, side, top]], axis=1),
                jnp.concatenate([kept[k, side, bottom], plain], axis=1),
            ],
            axis=0,
        )

    lax.fori_loop(0, kernels, build_cols, 0)

    lax.fori_loop(0, kernels, build_rows, 0)
    intensity[...] = jnp.zeros_like(intensity)
    descent[...] = jnp.zeros_like(descent)

    def receive(plane):
        for number, (down, right) in enumerate(DIRECTIONS):

            @pl.when(inside(down, right))
            def _():
                transfer(plane, number).wait_send()

            @pl.when(inside(-down, -right))
            def _():
                transfer(plane, number).wait_recv()

    receive(0)

    lanes = halo.shape[2]
    reach = rows + tile
    shifted = pltpu.roll(halo[0].astype(F32), lanes - two, 1)[:, :reach].astype(BF16)
    steps = wide // two
    for step in range(steps):
        windows[:, step * reach : (step + 1) * reach] = shifted[step * two : step * two + tile]

    batch = next(size for size in (4, 3, 2, 1) if kernels % size == 0)

    def col_pass(j, held):
        first = j * batch
        made = dot(
            col_mats[pl.ds(first, batch)].reshape(batch * parts * two, tile), windows[...]
        ).astype(BF16)
        for i in range(batch):
            for part in range(parts):
                top = (i * parts + part) * two
                for step in range(steps):
                    for band in range(bands + 1):
                        lane = step * reach + band * tile
                        held[
                            i,
                            band,
                            step * two : (step + 1) * two,
                            part * tile : (part + 1) * tile,
                        ] = made[top : top + two, lane : lane + tile]

    def row_pass(k, columns):
        weight = weight_ref[k]
        held = [columns[band] for band in range(bands + 1)]
        joined = jnp.concatenate(
            [jnp.concatenate(held[band : band + 2], axis=1) for band in range(bands)], axis=0
        )
        first, second = (square(row_mats, k, side, 1, 2) for side in range(2))
        whole = dot(joined, jnp.concatenate([first, second], axis=0))
        tail = dot(held[bands], first)
        for band in range(bands + 1):
            pair = tail if band == bands else whole[band * wide : (band + 1) * wide]
            fields[k, band] = pair.astype(BF16)
            real_part, imag_part = (pair[:, :tile], pair[:, tile:])
            intensity[band] += weight * (real_part * real_part + imag_part * imag_part)

    def row_passes(j, held):
        for i in range(batch):
            row_pass(j * batch + i, held.at[i])
            if i % 2 == 0:
                build_adjoints(j * batch + i)

    def in_pairs(make, take, count, helds):
        make(0, helds[0])
        size = next(size for size in (4, 2, 1) if count % size == 0)

        def step(j, final):
            for i in range(size):
                k = size * j + i
                ahead = not (final and i == size - 1)
                if size == 1:
                    take(k, helds[0])
                if ahead:
                    make(k + 1, helds[(i + 1) % 2 if size > 1 else 0])
                if size > 1:
                    take(k, helds[i % 2])

        def looped(j, carry):
            step(j, False)
            return carry

        lax.fori_loop(0, count // size - 1, looped, 0)
        step(count // size - 1, True)

    in_pairs(col_pass, row_passes, kernels // batch, (even_columns, odd_columns))

    swap = pltpu.make_async_remote_copy(
        src_ref=intensity,
        dst_ref=other,
        send_sem=expo_send,
        recv_sem=expo_recv,
        device_id={"expo": 1 - expo},
        device_id_type=MESH,
    )
    swap.start()

    def build_others(j, carry):
        for i in range(1, batch, 2):
            build_adjoints(j * batch + i)
        return carry

    lax.fori_loop(0, kernels // batch, build_others, 0)
    receive(1)
    swap.wait()

    def side_by_side(ref):
        return jnp.concatenate([ref[band] for band in range(bands + 1)], axis=1)

    total = side_by_side(intensity) + side_by_side(other)
    resist = jax.nn.sigmoid(resist_steep * (total - resist_level))
    target_ext = pltpu.roll(
        halo[1, half : half + wide, :].astype(F32), lanes - (tile - half), 1
    )[:, :reach]
    row_lanes = lax.broadcasted_iota(jnp.int32, (wide, reach), 1)
    row_ids = row_lanes + (strip * rows - half)
    col_ids = lax.broadcasted_iota(jnp.int32, (wide, reach), 0) + (col * width - half)
    kept = (
        (row_ids >= 0)
        & (row_ids < strips * rows)
        & (col_ids >= 0)
        & (col_ids < cols * width)
        & (row_lanes < rows + two)
    )
    mismatch = resist - target_ext
    steepness = jnp.where(kept, 2.0 * mismatch * resist_steep * resist * (1.0 - resist), 0.0)
    for band in range(bands + 1):
        slope[band] = steepness[:, band * tile : (band + 1) * tile]
    owned = (
        (row_lanes >= half)
        & (row_lanes < half + rows)
        & (col_ids >= col * width)
        & (col_ids < (col + 1) * width)
    )
    missed = jnp.sum(jnp.where(owned, mismatch * mismatch, 0.0), axis=0, keepdims=True)
    loss_line = sum(missed[:, band * tile : (band + 1) * tile] for band in range(bands + 1))
    shown[...] = resist[half : half + width, :]

    def correlate(k, held):
        scale = 2.0 * weight_ref[k]
        products = []
        for band in range(bands + 1):
            weighting = (scale * slope[band]).astype(BF16)
            products.append(fields[k, band] * jnp.concatenate([weighting] * parts, axis=1))
        joined = jnp.concatenate(
            [jnp.concatenate(products[band : band + 2], axis=1) for band in range(bands)], axis=0
        )
        matrix = jnp.concatenate(
            [square(row_adjoints, k, side, 2, 1) for side in range(2)], axis=0
        )
        returned = dot(joined, matrix).astype(BF16)
        for band in range(bands):
            held[band] = returned[band * wide : (band + 1) * wide]

    def correlate_all(j, held):
        for i in range(batch):
            correlate(j * batch + i, held.at[i])

    def gather_all(j, held):
        sources = []
        for i in range(batch):
            found = [
                jnp.concatenate(
                    [
                        held[i, band, :, part * tile : (part + 1) * tile]
                        for band in range(bands)
                    ],
                    axis=1,
                )
                for part in range(parts)
            ]
            sources += [f[:tile] for f in found] + [f[tile:] for f in found]
        matrix = jnp.concatenate([col_adjoints[j * batch + i] for i in range(batch)], axis=1)
        descent[...] += dot(matrix, jnp.concatenate(sources, axis=0))

    in_pairs(correlate_all, gather_all, kernels // batch, (even, odd))

    mask = jax.nn.sigmoid(mask_slope * params_ref[0])
    gradient = descent[...].T * mask_slope * mask * (1.0 - mask)
    steps_ref[...] = gradient
    square_line = jnp.sum(gradient * gradient, axis=0, keepdims=True)
    which = lax.broadcasted_iota(jnp.int32, partial.shape, 0)
    sums = jnp.where(which == 0, loss_line, jnp.where(which == 1, square_line, 0.0))
    partial[...] = sums
    slots[me] = sums

    shares, arrivals = ([], [])
    for number, (place, index) in enumerate(peers):
        for found, slot in ((shares, me), (arrivals, index)):
            found.append(
                pltpu.make_async_remote_copy(
                    src_ref=partial,
                    dst_ref=slots.at[slot],
                    send_sem=sum_send.at[number],
                    recv_sem=sum_recv.at[slot],
                    device_id=place,
                    device_id_type=MESH,
                )
            )
    for share in shares:
        share.start()
    resist_ref[...] = pltpu.roll(shown[...], reach - half, 1)[:, :rows].T

    for arrival in arrivals:
        arrival.wait()

    totals_ref[...] = jnp.sum(slots[...], axis=0)


def finish(copies, params_ref, steps_ref, resist_in, totals_ref, new_ref, resist_ref, loss_ref):
    expos, blocks = copies
    rows, width = steps_ref.shape
    pixels = rows * width * blocks
    loss_ref[0] = jnp.sum(totals_ref[0:1, :]) / (expos * pixels)
    square_sum = jnp.sum(totals_ref[1:2, :], axis=1, keepdims=True)
    root_mean = jnp.sqrt(square_sum / (expos * pixels) + norm_eps)
    new_ref[0] = params_ref[0] - step_length * steps_ref[...] / root_mean
    resist_ref[...] = resist_in[...]


def shards(mask_params, target, col_taps, row_taps, kernel_weights):
    rows, width = target.shape
    kernels, _, taps = col_taps.shape
    half = taps // 2
    two = 2 * half
    tile, wide, bands = (2 * two, width + two, rows // (2 * two))
    strips, cols, expos = (lax.axis_size(a) for a in ("strip", "col", "expo"))
    group = strips * cols * expos
    vmem = pl.BlockSpec(memory_space=pltpu.VMEM)
    smem = pl.BlockSpec(memory_space=pltpu.SMEM)
    dma = pltpu.SemaphoreType.DMA
    image = jax.ShapeDtypeStruct(target.shape, F32)
    batch = next(size for size in (4, 3, 2, 1) if kernels % size == 0)
    anywhere = pl.BlockSpec(memory_space=pltpu.HBM)
    steps, resist, totals = pl.pallas_call(
        functools.partial(body, (strips, cols, expos, half)),
        out_shape=(image, image, jax.ShapeDtypeStruct((8, width), F32)),
        in_specs=[anywhere] * 5,
        out_specs=(vmem, vmem, vmem),
        scratch_shapes=[
            pltpu.VMEM(mask_params.shape, F32),
            pltpu.VMEM(target.shape, target.dtype),
            pltpu.VMEM(col_taps.shape, col_taps.dtype),
            pltpu.VMEM(row_taps.shape, row_taps.dtype),
            pltpu.SMEM(kernel_weights.shape, F32),
            pltpu.VMEM((2, width + 2 * two, rows + 2 * tile), BF16),
            pltpu.VMEM((tile, (wide // two) * (rows + tile)), BF16),
            pltpu.VMEM((2, 2 * kernels, tile), F32),
            pltpu.VMEM((3, 2 * kernels, tile), F32),
            pltpu.VMEM((4, tile, tile), BF16),
            pltpu.VMEM((kernels, 2 * two, tile), BF16),
            pltpu.VMEM((kernels, 2, 3, tile, tile), BF16),
            pltpu.VMEM((kernels, 2, 3, tile, tile), BF16),
            pltpu.VMEM((kernels, width, 3 * tile), BF16),
            pltpu.VMEM((batch, bands + 1, wide, 2 * tile), BF16),
            pltpu.VMEM((batch, bands + 1, wide, 2 * tile), BF16),
            pltpu.VMEM((kernels, bands + 1, wide, 2 * tile), BF16),
            pltpu.VMEM((bands + 1, wide, tile), F32),
            pltpu.VMEM((bands + 1, wide, tile), F32),
            pltpu.VMEM((bands + 1, wide, tile), F32),
            pltpu.VMEM((batch, bands, wide, 2 * tile), BF16),
            pltpu.VMEM((batch, bands, wide, 2 * tile), BF16),
            pltpu.VMEM((width, rows), F32),
            pltpu.VMEM((width, rows + tile), F32),
            pltpu.VMEM((8, width), F32),
            pltpu.VMEM((group, 8, width), F32),
            dma((5,)),
            dma((2, 8)),
            dma((2, 8)),
            dma,
            dma,
            dma((group,)),
            dma((group,)),
        ],
        compiler_params=pltpu.CompilerParams(
            collective_id=0, has_side_effects=True, vmem_limit_bytes=40 * 1024 * 1024
        ),
    )(mask_params, target, col_taps, row_taps, kernel_weights)
    return pl.pallas_call(
        functools.partial(finish, (expos, strips * cols)),
        out_shape=(
            jax.ShapeDtypeStruct(mask_params.shape, F32),
            image,
            jax.ShapeDtypeStruct((1,), F32),
        ),
        in_specs=[vmem] * 4,
        out_specs=(vmem, vmem, smem),
    )(mask_params, steps, resist, totals)


def solution(mesh):
    return jax.shard_map(
        shards,
        mesh=mesh,
        in_specs=(
            P("expo", ("tiles", "strip"), "col"),
            P(("tiles", "strip"), "col"),
            P(),
            P(),
            P(),
        ),
        out_specs=(P("expo", ("tiles", "strip"), "col"), P(("tiles", "strip"), "col"), P("tiles")),
        check_vma=False,
    )
```

```python
import functools

import jax
import jax.numpy as jnp
from jax import lax
from jax.experimental import pallas as pl
from jax.experimental.pallas import tpu as pltpu
from jax.sharding import PartitionSpec as P

mask_slope = 4.0
resist_steep = 4.0
resist_level = 3.0
step_length = 0.5
norm_eps = 1e-06

MESH = pl.DeviceIdType.MESH
F32 = jnp.float32
BF16 = jnp.bfloat16
DIRECTIONS = [(a, b) for a in (-1, 0, 1) for b in (-1, 0, 1) if (a, b) != (0, 0)]


def dot(a, b):
    return jnp.dot(a, b, preferred_element_type=F32)


def body(
    sizes,
    params_hbm,
    target_hbm,
    col_hbm,
    row_hbm,
    weight_hbm,
    steps_ref,
    resist_ref,
    totals_ref,
    params_ref,
    target_ref,
    col_ref,
    row_ref,
    weight_ref,
    halo,
    windows,
    padded,
    lines,
    masks,
    col_mats,
    row_mats,
    row_adjoints,
    col_adjoints,
    even_columns,
    odd_columns,
    fields,
    intensity,
    other,
    slope,
    even,
    odd,
    descent,
    shown,
    partial,
    slots,
    fetch_sem,
    halo_send,
    halo_recv,
    expo_send,
    expo_recv,
    sum_send,
    sum_recv,
):
    strips, cols, expos, half = sizes
    kernels, parts, taps = col_ref.shape
    rows, width = target_ref.shape
    two = 2 * half
    tile = 2 * two
    wide = width + two
    bands = rows // tile
    group = strips * cols * expos
    strip, col, expo = (lax.axis_index("strip"), lax.axis_index("col"), lax.axis_index("expo"))
    me = (strip * cols + col) * expos + expo

    def beyond(index, step, count):
        moved = index + step
        return jnp.where(moved >= count, moved - count, moved)

    peers = []
    for number in range(1, group):
        steps_to = (number // (cols * expos), number // expos % cols, number % expos)
        there = [
            beyond(index, step, count) if step else index
            for index, step, count in zip((strip, col, expo), steps_to, sizes[:3])
        ]
        peers.append(
            (
                dict(zip(("strip", "col", "expo"), there)),
                (there[0] * cols + there[1]) * expos + there[2],
            )
        )

    fetches = [
        pltpu.make_async_copy(source, into, fetch_sem.at[number])
        for number, (source, into) in enumerate(
            (
                (params_hbm, params_ref),
                (target_hbm, target_ref),
                (col_hbm, col_ref),
                (row_hbm, row_ref),
                (weight_hbm, weight_ref),
            )
        )
    ]
    for fetch in fetches:
        fetch.start()

    halo[...] = jnp.zeros_like(halo)

    barrier = pltpu.get_barrier_semaphore()

    for place, _ in peers:
        pl.semaphore_signal(barrier, inc=1, device_id=place, device_id_type=MESH)

    for fetch in fetches[:2]:
        fetch.wait()
    mask = jax.nn.sigmoid(mask_slope * params_ref[0])
    halo[0, two : two + width, tile : tile + rows] = mask.T.astype(BF16)
    target_now = target_ref[...].astype(F32)
    halo[1, two : two + width, tile : tile + rows] = target_now.T.astype(BF16)

    def transfer(plane, number):
        down, right = DIRECTIONS[number]
        lane, lanes, to_lane = {
            -1: (tile, tile, tile + rows),
            0: (tile, rows, tile),
            1: (rows, tile, 0),
        }[down]
        place, places, to_place = {
            -1: (two, two, two + width),
            0: (two, width, two),
            1: (width, two, 0),
        }[right]
        return pltpu.make_async_remote_copy(
            src_ref=halo.at[plane, pl.ds(place, places), pl.ds(lane, lanes)],
            dst_ref=halo.at[plane, pl.ds(to_place, places), pl.ds(to_lane, lanes)],
            send_sem=halo_send.at[plane, number],
            recv_sem=halo_recv.at[plane, number],
            device_id={
                "strip": jnp.clip(strip + down, 0, strips - 1),
                "col": jnp.clip(col + right, 0, cols - 1),
            },
            device_id_type=MESH,
        )

    def inside(down, right):
        to_strip, to_col = (strip + down, col + right)
        return (to_strip >= 0) & (to_strip < strips) & (to_col >= 0) & (to_col < cols)

    pl.semaphore_wait(barrier, group - 1)

    for plane in range(2):
        for number, (down, right) in enumerate(DIRECTIONS):

            @pl.when(inside(down, right))
            def _():
                transfer(plane, number).start()

    for fetch in fetches[2:]:
        fetch.wait()
    padded[...] = jnp.zeros_like(padded)
    for k in range(kernels):
        for table, source in enumerate((col_ref, row_ref)):
            padded[table, parts * k : parts * (k + 1), :taps] = source[k].astype(F32)
    tap_ids = lax.broadcasted_iota(jnp.int32, (tile, tile), 0)
    places = lax.broadcasted_iota(jnp.int32, (tile, tile), 1)

    def chosen(flags):
        return jnp.where(flags, 1.0, 0.0).astype(BF16)

    col_lines, row_lines = (padded[0].astype(BF16), padded[1].astype(BF16))
    last = taps - 1
    lines[0] = dot(row_lines, chosen((tap_ids + places == tile) | (tap_ids + places == 0)))
    lines[1] = dot(
        row_lines, chosen((places - tap_ids == tile - last) | (tap_ids - places == last))
    )
    lines[2] = dot(col_lines, chosen(tap_ids + places == last))
    masks[0] = chosen(tap_ids >= places)
    masks[1] = chosen(tap_ids < places)
    masks[2] = chosen(tap_ids <= places)
    masks[3] = chosen(tap_ids > jnp.where(places < two, places, places - two))

    def rolled(line, count):
        return pltpu.roll(
            jnp.broadcast_to(line, (count, tile)), 0, 1, stride=1, stride_axis=0
        )

    def circulant(table, k, part):
        return rolled(lines[table, pl.ds(parts * k + part, 1), :], tile)

    def build_cols(k, carry):
        for part in range(parts):
            line = padded[0, pl.ds(parts * k + part, 1), :]
            col_mats[k, part * two : (part + 1) * two, :] = rolled(line, two).astype(BF16)
        return carry

    def triangles(table, k, kept):
        t0, t1 = (circulant(table, k, part).astype(BF16) for part in range(parts))
        for side in range(2):
            a1 = t1 * masks[side]
            kept[k, side, 0] = t0 * masks[side]
            kept[k, side, 1] = a1
            kept[k, side, 2] = -a1

    def build_rows(k, carry):
        triangles(0, k, row_mats)
        return carry

    def build_adjoints(k):
        triangles(1, k, row_adjoints)
        u0, u1 = (circulant(2, k, part) for part in range(parts))
        col_adjoints[k, :, :tile] = u0.astype(BF16) * masks[2]
        col_adjoints[k, :, tile : 2 * tile] = u1.astype(BF16) * masks[2]
        mixed = jnp.where(places < two, u0, pltpu.roll(u1, two, 1)).astype(BF16)
        col_adjoints[k, :, 2 * tile :] = mixed * masks[3]

    def square(kept, k, side, top, bottom):
        plain = kept[k, side, 0]
        return jnp.concatenate(
            [
                jnp.concatenate([plain, kept[k, side, top]], axis=1),
                jnp.concatenate([kept[k, side, bottom], plain], axis=1),
            ],
            axis=0,
        )

    lax.fori_loop(0, kernels, build_cols, 0)

    lax.fori_loop(0, kernels, build_rows, 0)
    intensity[...] = jnp.zeros_like(intensity)
    descent[...] = jnp.zeros_like(descent)

    def receive(plane):
        for number, (down, right) in enumerate(DIRECTIONS):

            @pl.when(inside(down, right))
            def _():
                transfer(plane, number).wait_send()

            @pl.when(inside(-down, -right))
            def _():
                transfer(plane, number).wait_recv()

    receive(0)

    lanes = halo.shape[2]
    reach = rows + tile
    shifted = pltpu.roll(halo[0].astype(F32), lanes - two, 1)[:, :reach].astype(BF16)
    steps = wide // two
    for step in range(steps):
        windows[:, step * reach : (step + 1) * reach] = shifted[step * two : step * two + tile]

    batch = next(size for size in (4, 3, 2, 1) if kernels % size == 0)

    def col_pass(j, held):
        first = j * batch
        made = dot(
            col_mats[pl.ds(first, batch)].reshape(batch * parts * two, tile), windows[...]
        ).astype(BF16)
        for i in range(batch):
            for part in range(parts):
                top = (i * parts + part) * two
                for step in range(steps):
                    for band in range(bands + 1):
                        lane = step * reach + band * tile
                        held[
                            i,
                            band,
                            step * two : (step + 1) * two,
                            part * tile : (part + 1) * tile,
                        ] = made[top : top + two, lane : lane + tile]

    def row_pass(k, columns):
        weight = weight_ref[k]
        held = [columns[band] for band in range(bands + 1)]
        joined = jnp.concatenate(
            [jnp.concatenate(held[band : band + 2], axis=1) for band in range(bands)], axis=0
        )
        first, second = (square(row_mats, k, side, 1, 2) for side in range(2))
        whole = dot(joined, jnp.concatenate([first, second], axis=0))
        tail = dot(held[bands], first)
        for band in range(bands + 1):
            pair = tail if band == bands else whole[band * wide : (band + 1) * wide]
            fields[k, band] = pair.astype(BF16)
            real_part, imag_part = (pair[:, :tile], pair[:, tile:])
            intensity[band] += weight * (real_part * real_part + imag_part * imag_part)

    def row_passes(j, held):
        for i in range(batch):
            row_pass(j * batch + i, held.at[i])
            if i % 2 == 0:
                build_adjoints(j * batch + i)

    def in_pairs(make, take, count, helds):
        make(0, helds[0])
        size = next(size for size in (4, 2, 1) if count % size == 0)

        def step(j, final):
            for i in range(size):
                k = size * j + i
                ahead = not (final and i == size - 1)
                if size == 1:
                    take(k, helds[0])
                if ahead:
                    make(k + 1, helds[(i + 1) % 2 if size > 1 else 0])
                if size > 1:
                    take(k, helds[i % 2])

        def looped(j, carry):
            step(j, False)
            return carry

        lax.fori_loop(0, count // size - 1, looped, 0)
        step(count // size - 1, True)

    in_pairs(col_pass, row_passes, kernels // batch, (even_columns, odd_columns))

    swap = pltpu.make_async_remote_copy(
        src_ref=intensity,
        dst_ref=other,
        send_sem=expo_send,
        recv_sem=expo_recv,
        device_id={"expo": 1 - expo},
        device_id_type=MESH,
    )
    swap.start()

    def build_others(j, carry):
        for i in range(1, batch, 2):
            build_adjoints(j * batch + i)
        return carry

    lax.fori_loop(0, kernels // batch, build_others, 0)
    receive(1)
    swap.wait()

    def side_by_side(ref):
        return jnp.concatenate([ref[band] for band in range(bands + 1)], axis=1)

    total = side_by_side(intensity) + side_by_side(other)
    resist = jax.nn.sigmoid(resist_steep * (total - resist_level))
    target_ext = pltpu.roll(
        halo[1, half : half + wide, :].astype(F32), lanes - (tile - half), 1
    )[:, :reach]
    row_lanes = lax.broadcasted_iota(jnp.int32, (wide, reach), 1)
    row_ids = row_lanes + (strip * rows - half)
    col_ids = lax.broadcasted_iota(jnp.int32, (wide, reach), 0) + (col * width - half)
    kept = (
        (row_ids >= 0)
        & (row_ids < strips * rows)
        & (col_ids >= 0)
        & (col_ids < cols * width)
        & (row_lanes < rows + two)
    )
    mismatch = resist - target_ext
    steepness = jnp.where(kept, 2.0 * mismatch * resist_steep * resist * (1.0 - resist), 0.0)
    for band in range(bands + 1):
        slope[band] = steepness[:, band * tile : (band + 1) * tile]
    owned = (
        (row_lanes >= half)
        & (row_lanes < half + rows)
        & (col_ids >= col * width)
        & (col_ids < (col + 1) * width)
    )
    missed = jnp.sum(jnp.where(owned, mismatch * mismatch, 0.0), axis=0, keepdims=True)
    loss_line = sum(missed[:, band * tile : (band + 1) * tile] for band in range(bands + 1))
    shown[...] = resist[half : half + width, :]

    def correlate(k, held):
        scale = 2.0 * weight_ref[k]
        products = []
        for band in range(bands + 1):
            weighting = (scale * slope[band]).astype(BF16)
            products.append(fields[k, band] * jnp.concatenate([weighting] * parts, axis=1))
        joined = jnp.concatenate(
            [jnp.concatenate(products[band : band + 2], axis=1) for band in range(bands)], axis=0
        )
        matrix = jnp.concatenate(
            [square(row_adjoints, k, side, 2, 1) for side in range(2)], axis=0
        )
        returned = dot(joined, matrix).astype(BF16)
        for band in range(bands):
            held[band] = returned[band * wide : (band + 1) * wide]

    def correlate_all(j, held):
        for i in range(batch):
            correlate(j * batch + i, held.at[i])

    def gather_all(j, held):
        sources = []
        for i in range(batch):
            found = [
                jnp.concatenate(
                    [
                        held[i, band, :, part * tile : (part + 1) * tile]
                        for band in range(bands)
                    ],
                    axis=1,
                )
                for part in range(parts)
            ]
            sources += [f[:tile] for f in found] + [f[tile:] for f in found]
        matrix = jnp.concatenate([col_adjoints[j * batch + i] for i in range(batch)], axis=1)
        descent[...] += dot(matrix, jnp.concatenate(sources, axis=0))

    in_pairs(correlate_all, gather_all, kernels // batch, (even, odd))

    mask = jax.nn.sigmoid(mask_slope * params_ref[0])
    gradient = descent[...].T * mask_slope * mask * (1.0 - mask)
    steps_ref[...] = gradient
    square_line = jnp.sum(gradient * gradient, axis=0, keepdims=True)
    which = lax.broadcasted_iota(jnp.int32, partial.shape, 0)
    sums = jnp.where(which == 0, loss_line, jnp.where(which == 1, square_line, 0.0))
    partial[...] = sums
    slots[me] = sums

    shares, arrivals = ([], [])
    for number, (place, index) in enumerate(peers):
        for found, slot in ((shares, me), (arrivals, index)):
            found.append(
                pltpu.make_async_remote_copy(
                    src_ref=partial,
                    dst_ref=slots.at[slot],
                    send_sem=sum_send.at[number],
                    recv_sem=sum_recv.at[slot],
                    device_id=place,
                    device_id_type=MESH,
                )
            )
    for share in shares:
        share.start()
    resist_ref[...] = pltpu.roll(shown[...], reach - half, 1)[:, :rows].T

    for arrival in arrivals:
        arrival.wait()

    totals_ref[...] = jnp.sum(slots[...], axis=0)


def finish(copies, params_ref, steps_ref, resist_in, totals_ref, new_ref, resist_ref, loss_ref):
    expos, blocks = copies
    rows, width = steps_ref.shape
    pixels = rows * width * blocks
    loss_ref[0] = jnp.sum(totals_ref[0:1, :]) / (expos * pixels)
    square_sum = jnp.sum(totals_ref[1:2, :], axis=1, keepdims=True)
    root_mean = jnp.sqrt(square_sum / (expos * pixels) + norm_eps)
    new_ref[0] = params_ref[0] - step_length * steps_ref[...] / root_mean
    resist_ref[...] = resist_in[...]


def shards(mask_params, target, col_taps, row_taps, kernel_weights):
    rows, width = target.shape
    kernels, _, taps = col_taps.shape
    half = taps // 2
    two = 2 * half
    tile, wide, bands = (2 * two, width + two, rows // (2 * two))
    strips, cols, expos = (lax.axis_size(a) for a in ("strip", "col", "expo"))
    group = strips * cols * expos
    vmem = pl.BlockSpec(memory_space=pltpu.VMEM)
    smem = pl.BlockSpec(memory_space=pltpu.SMEM)
    dma = pltpu.SemaphoreType.DMA
    image = jax.ShapeDtypeStruct(target.shape, F32)
    batch = next(size for size in (4, 3, 2, 1) if kernels % size == 0)
    anywhere = pl.BlockSpec(memory_space=pltpu.HBM)
    steps, resist, totals = pl.pallas_call(
        functools.partial(body, (strips, cols, expos, half)),
        out_shape=(image, image, jax.ShapeDtypeStruct((8, width), F32)),
        in_specs=[anywhere] * 5,
        out_specs=(vmem, vmem, vmem),
        scratch_shapes=[
            pltpu.VMEM(mask_params.shape, F32),
            pltpu.VMEM(target.shape, target.dtype),
            pltpu.VMEM(col_taps.shape, col_taps.dtype),
            pltpu.VMEM(row_taps.shape, row_taps.dtype),
            pltpu.SMEM(kernel_weights.shape, F32),
            pltpu.VMEM((2, width + 2 * two, rows + 2 * tile), BF16),
            pltpu.VMEM((tile, (wide // two) * (rows + tile)), BF16),
            pltpu.VMEM((2, 2 * kernels, tile), F32),
            pltpu.VMEM((3, 2 * kernels, tile), F32),
            pltpu.VMEM((4, tile, tile), BF16),
            pltpu.VMEM((kernels, 2 * two, tile), BF16),
            pltpu.VMEM((kernels, 2, 3, tile, tile), BF16),
            pltpu.VMEM((kernels, 2, 3, tile, tile), BF16),
            pltpu.VMEM((kernels, width, 3 * tile), BF16),
            pltpu.VMEM((batch, bands + 1, wide, 2 * tile), BF16),
            pltpu.VMEM((batch, bands + 1, wide, 2 * tile), BF16),
            pltpu.VMEM((kernels, bands + 1, wide, 2 * tile), BF16),
            pltpu.VMEM((bands + 1, wide, tile), F32),
            pltpu.VMEM((bands + 1, wide, tile), F32),
            pltpu.VMEM((bands + 1, wide, tile), F32),
            pltpu.VMEM((batch, bands, wide, 2 * tile), BF16),
            pltpu.VMEM((batch, bands, wide, 2 * tile), BF16),
            pltpu.VMEM((width, rows), F32),
            pltpu.VMEM((width, rows + tile), F32),
            pltpu.VMEM((8, width), F32),
            pltpu.VMEM((group, 8, width), F32),
            dma((5,)),
            dma((2, 8)),
            dma((2, 8)),
            dma,
            dma,
            dma((group,)),
            dma((group,)),
        ],
        compiler_params=pltpu.CompilerParams(
            collective_id=0, has_side_effects=True, vmem_limit_bytes=56 * 1024 * 1024
        ),
    )(mask_params, target, col_taps, row_taps, kernel_weights)
    return pl.pallas_call(
        functools.partial(finish, (expos, strips * cols)),
        out_shape=(
            jax.ShapeDtypeStruct(mask_params.shape, F32),
            image,
            jax.ShapeDtypeStruct((1,), F32),
        ),
        in_specs=[vmem] * 4,
        out_specs=(vmem, vmem, smem),
    )(mask_params, steps, resist, totals)


def solution(mesh):
    return jax.shard_map(
        shards,
        mesh=mesh,
        in_specs=(
            P("expo", ("tiles", "strip"), "col"),
            P(("tiles", "strip"), "col"),
            P(),
            P(),
            P(),
        ),
        out_specs=(P("expo", ("tiles", "strip"), "col"), P(("tiles", "strip"), "col"), P("tiles")),
        check_vma=False,
    )
```
